256 devices in a mesh: dp: 128 (over y_lo, z, x, core), section: 2 (over y_hi).
Axes of the slice: x: 4, y: 4 (y_hi: 2, y_lo: 2; y = y_hi * 2 + y_lo), z: 8, core: 2. Of those that a mesh axis runs over, the one named last changes fastest.
Arguments:
- teacher_image: bfloat16 [65536, 1536], P(('dp', 'section')), may hold values from -6 to 6
- teacher_proj: bfloat16 [1536, 1536], replicated, may hold values from -0.15625 to 0.15625
- teacher_text: bfloat16 [65536, 1536], P(('dp', 'section')), may hold values from -6 to 6
- image_feats: bfloat16 [65536, 768], P(('dp', 'section')), may hold values from -6 to 6
- text_feats: bfloat16 [65536, 768], P(('dp', 'section')), may hold values from -6 to 6
- image_proj: bfloat16 [768, 768], replicated, may hold values from -0.21875 to 0.21875
- text_proj: bfloat16 [768, 768], replicated, may hold values from -0.21875 to 0.21875
- class_ids: int32 [65536], P(('dp', 'section')), may hold values from 0 to 255
Outputs:
- grad_image_proj: float32 [768, 768], replicated
- grad_text_proj: float32 [768, 768], replicated
The draws below stay inside these ranges and needn't reach their ends.
All inputs are finite; a program needn't handle non-finite values.
Results may differ from the reference program's by a relative error of at most 0.005.
Values may be sent and summed in bfloat16 or wider, within the bound.
No kernel may reach another device: no remote copies, remote signals or barrier semaphores. Data moves between devices by JAX's collectives and lax.ppermute only.
A program may use at most 128 MiB of HBM per device.

```python
import jax
import jax.numpy as jnp
from jax import lax

DS = 768
DT = 1536
ROWS = 256
WINDOW = 4
NCLASS = 256
BATCH = 65536
N_DP = 128


def with_ends(array, key, least, top_value):
    spot = [jax.random.randint(jax.random.fold_in(key, axis), (), 0, length) for axis, length in enumerate(array.shape)]
    widest = array.shape.index(max(array.shape))
    beside = spot[:widest] + [(spot[widest] + 1) % array.shape[widest]] + spot[widest + 1:]
    return array.at[tuple(spot)].set(least).at[tuple(beside)].set(top_value)


def level_of(key, shape, cuts, low, largest):
    gain, own = 1.0, jax.random.fold_in(key, 6)
    for dim, shards_of in cuts:
        heights = jnp.exp(jax.random.uniform(jax.random.fold_in(own, dim), (shards_of,), jnp.float32, low / len(cuts), largest / len(cuts)))
        gain = gain * jnp.repeat(heights, shape[dim] // shards_of).reshape([-1 if axis == dim else 1 for axis in range(len(shape))])
    return gain


def bell_draw(own_key, shape, deviation, bound, pieces=(), kind=jnp.bfloat16):
    gain = level_of(own_key, shape, pieces, -0.22, 0.18) if pieces else 1.0
    result = jax.random.normal(own_key, shape, jnp.float32) * deviation * gain
    return jnp.minimum(jnp.maximum(result, -bound), bound).astype(kind)


def setup_inputs(seed: int = 0) -> dict:
    key_of = jax.random.split(jax.random.key(seed), 9)
    return {
        "teacher_image": bell_draw(key_of[0], (BATCH, DT), 1.0, 6.0, ((0, 256),)),
        "teacher_proj": bell_draw(key_of[1], (DT, DT), DT ** -0.5, 0.15625),
        "teacher_text": bell_draw(key_of[2], (BATCH, DT), 1.0, 6.0, ((0, 256),)),
        "image_feats": bell_draw(key_of[3], (BATCH, DS), 1.0, 6.0, ((0, 256),)),
        "text_feats": bell_draw(key_of[4], (BATCH, DS), 1.0, 6.0, ((0, 256),)),
        "image_proj": bell_draw(key_of[5], (DS, DS), DS ** -0.5, 0.21875),
        "text_proj": bell_draw(key_of[6], (DS, DS), DS ** -0.5, 0.21875),
        "class_ids": with_ends(jax.random.randint(key_of[7], (BATCH,), 0, NCLASS), jax.random.fold_in(key_of[7], 1), 0, NCLASS - 1).astype(jnp.int32),
    }


epsilon = 1e-06
teacher_scale = 20.0
teacher_shift = -1.0
student_scale = 20.0
student_shift = -1.0

def unit_rows(raw_rows):
    row_len = jnp.sqrt(lax.optimization_barrier(jnp.sum(raw_rows * raw_rows, axis=1, keepdims=True)) + epsilon)
    return (raw_rows / row_len, row_len)

def pair_tile(teach_rows, image_rows, row_ids, teach_cols, text_cols, col_ids):
    teacher_dot = lax.dot_general(teach_rows, teach_cols, (((1,), (1,)), ((), ())), preferred_element_type=jnp.float32)
    labels = (row_ids[:, None] == col_ids[None, :]).astype(jnp.float32)
    target = 0.5 * jax.nn.sigmoid(teacher_scale * teacher_dot + teacher_shift) + 0.5 * labels
    logits = student_scale * lax.dot_general(image_rows, text_cols, (((1,), (1,)), ((), ())), preferred_element_type=jnp.float32) + student_shift
    scaled = ((jax.nn.sigmoid(logits) - target) / ROWS).astype(jnp.bfloat16)
    row_part = student_scale * jnp.dot(scaled, text_cols, preferred_element_type=jnp.float32)
    col_part = student_scale * lax.dot_general(scaled, image_rows, (((0,), (0,)), ((), ())), preferred_element_type=jnp.float32)
    return (row_part, col_part)

def weight_grad(feats, unit, length, grad):
    direction = (grad - unit * lax.optimization_barrier(jnp.sum(unit * grad, axis=1, keepdims=True))) / length
    high = direction.astype(jnp.bfloat16)
    low = (direction - high.astype(jnp.float32)).astype(jnp.bfloat16)
    dims = (((0,), (0,)), ((), ()))
    first = lax.dot_general(feats, high, dims, preferred_element_type=jnp.float32)
    second = lax.dot_general(feats, low, dims, preferred_element_type=jnp.float32)
    return first + second

def reference(teacher_image, teacher_proj, teacher_text, image_feats, text_feats, image_proj, text_proj, class_ids):
    teacher_unit, teacher_len = unit_rows(jnp.dot(teacher_image, teacher_proj, preferred_element_type=jnp.float32))
    teacher_img = teacher_unit.astype(jnp.bfloat16)
    written_unit, written_len = unit_rows(teacher_text.astype(jnp.float32))
    teacher_txt = written_unit.astype(jnp.bfloat16)
    image_unit, image_len = unit_rows(jnp.dot(image_feats, image_proj, preferred_element_type=jnp.float32))
    text_unit, text_len = unit_rows(jnp.dot(text_feats, text_proj, preferred_element_type=jnp.float32))
    image_emb = image_unit.astype(jnp.bfloat16)
    text_emb = text_unit.astype(jnp.bfloat16)

    def per_block(grad_txt, block):
        start = (block * (2 * ROWS)).astype(jnp.int32)
        teach_rows = lax.dynamic_slice_in_dim(teacher_img, start, 2 * ROWS, 0)
        image_rows = lax.dynamic_slice_in_dim(image_emb, start, 2 * ROWS, 0)
        row_ids = lax.dynamic_slice_in_dim(class_ids, start, 2 * ROWS, 0)
        grad_rows = jnp.zeros((2 * ROWS, DS), jnp.float32)
        for offset in range(WINDOW):
            for half in range(2):
                col_start = (((block - offset) % N_DP * 2 + half) * ROWS).astype(jnp.int32)
                teach_cols = lax.dynamic_slice_in_dim(teacher_txt, col_start, ROWS, 0)
                text_cols = lax.dynamic_slice_in_dim(text_emb, col_start, ROWS, 0)
                col_ids = lax.dynamic_slice_in_dim(class_ids, col_start, ROWS, 0)
                row_part, col_part = pair_tile(teach_rows, image_rows, row_ids, teach_cols, text_cols, col_ids)
                grad_rows = grad_rows + row_part
                before = lax.dynamic_slice_in_dim(grad_txt, col_start, ROWS, 0)
                grad_txt = lax.dynamic_update_slice_in_dim(grad_txt, before + col_part, col_start, 0)
        return (grad_txt, grad_rows)
    grad_txt, grad_blocks = lax.scan(per_block, jnp.zeros((BATCH, DS), jnp.float32), jnp.arange(N_DP, dtype=jnp.int32))
    grad_img = grad_blocks.reshape(BATCH, DS)
    grad_image_proj = weight_grad(image_feats, image_unit, image_len, grad_img)
    grad_text_proj = weight_grad(text_feats, text_unit, text_len, grad_txt)
    return (grad_image_proj, grad_text_proj)
```

```python
import jax
import jax.numpy as jnp
from jax import lax
from jax.sharding import Mesh
from jax.sharding import PartitionSpec as P

epsilon = 1e-06
scale = 20.0
shift = -1.0

AXES = ("yl", "z", "x", "core", "yh")
DP = ("yl", "z", "x", "core")
N_DP = 128

f32 = jnp.float32
bf16 = jnp.bfloat16


def unit_rows(raw_rows):
    row_len = jnp.sqrt(jnp.sum(raw_rows * raw_rows, axis=1, keepdims=True) + epsilon)
    return (raw_rows / row_len, row_len)


def swap(block, axis):
    return lax.ppermute(block, axis, [(0, 1), (1, 0)])


def along_dp(block, route):
    return lax.ppermute(block, DP, route)


def chip_shift(block, step):
    return along_dp(block, [(i, (i + 2 * step) % N_DP) for i in range(N_DP)])


def pair_tile(target_rows, image_rows, row_ids, target_cols, text_cols, col_ids):
    teacher_dot = lax.dot_general(
        target_rows, target_cols, (((1,), (1,)), ((), ())), preferred_element_type=f32
    )
    labels = (row_ids[:, None] == col_ids[None, :]).astype(f32)
    target = 0.5 * jax.nn.sigmoid(scale * teacher_dot + shift) + 0.5 * labels
    logits = (
        scale
        * lax.dot_general(
            image_rows, text_cols, (((1,), (1,)), ((), ())), preferred_element_type=f32
        )
        + shift
    )
    scaled = ((jax.nn.sigmoid(logits) - target) / text_cols.shape[0]).astype(bf16)
    row_part = scale * jnp.dot(scaled, text_cols, preferred_element_type=f32)
    col_part = scale * lax.dot_general(
        scaled, image_rows, (((0,), (0,)), ((), ())), preferred_element_type=f32
    )
    return (row_part, col_part)


def direction(unit, length, grad):
    d = (grad - unit * jnp.sum(unit * grad, axis=1, keepdims=True)) / length
    high = d.astype(bf16)
    low = (d - high.astype(f32)).astype(bf16)
    return high, low


def local(
    teacher_image,
    teacher_proj,
    teacher_text,
    image_feats,
    text_feats,
    image_proj,
    text_proj,
    class_ids,
):
    core = lax.axis_index("core")
    first = core == 0
    back_route = [(i, i - 1 if i % 2 else (i - 3) % N_DP) for i in range(N_DP)]
    step_route = [(i, (i + 1) % N_DP) for i in range(N_DP)]

    ids_y = swap(class_ids, "yh")
    ids1 = along_dp(class_ids, step_route)
    ids2 = along_dp(class_ids, [(i, (i + 2) % N_DP) for i in range(N_DP)])
    ids3 = along_dp(class_ids, [(i, (i + 3) % N_DP) for i in range(N_DP)])

    text_unit, text_len = unit_rows(jnp.dot(text_feats, text_proj, preferred_element_type=f32))
    text_emb = text_unit.astype(bf16)
    text_recv = chip_shift(text_emb, 1)
    image_unit, image_len = unit_rows(
        jnp.dot(image_feats, image_proj, preferred_element_type=f32)
    )
    image_emb = image_unit.astype(bf16)
    image_y = swap(image_emb, "yh")
    written_unit, _ = unit_rows(teacher_text.astype(f32))
    teacher_txt = written_unit.astype(bf16)
    teach_recv = chip_shift(teacher_txt, 1)
    teacher_unit, _ = unit_rows(jnp.dot(teacher_image, teacher_proj, preferred_element_type=f32))
    teacher_img = teacher_unit.astype(bf16)
    teach_y = swap(teacher_img, "yh")
    text_exch = swap(text_recv, "core")
    text_far = along_dp(jnp.where(first, text_emb, text_recv), step_route)
    teach_exch = swap(teach_recv, "core")
    teach_far = along_dp(jnp.where(first, teacher_txt, teach_recv), step_route)

    sent_feats = jnp.where(first, text_feats, image_feats)
    kept_feats = jnp.where(first, image_feats, text_feats)
    feats_in = swap(sent_feats, "core")

    image_rows = jnp.concatenate([image_emb, image_y], axis=0)
    teach_rows = jnp.concatenate([teacher_img, teach_y], axis=0)
    row_ids = jnp.concatenate([class_ids, ids_y], axis=0)
    row0, col0 = pair_tile(teach_rows, image_rows, row_ids, teacher_txt, text_emb, class_ids)
    row1, col1 = pair_tile(teach_rows, image_rows, row_ids, teach_recv, text_recv, ids2)
    ids_exch = jnp.where(first, ids1, ids3)
    row2, col2 = pair_tile(teach_rows, image_rows, row_ids, teach_exch, text_exch, ids_exch)
    both = col1 + swap(col2.astype(bf16), "core").astype(f32)
    both_back = chip_shift(both.astype(bf16), -1)
    ids_far = jnp.where(first, ids3, ids1)
    row3, col3 = pair_tile(teach_rows, image_rows, row_ids, teach_far, text_far, ids_far)
    far_back = along_dp(col3.astype(bf16), back_route)
    grad_rows = row0 + row1 + row2 + row3
    half = text_emb.shape[0]
    rows_y = swap(grad_rows[half:].astype(bf16), "yh")
    grad_img = grad_rows[:half] + rows_y.astype(f32)
    grad_txt = col0 + both_back.astype(f32) + far_back.astype(f32)

    img_high, img_low = direction(image_unit, image_len, grad_img)
    txt_high, txt_low = direction(text_unit, text_len, grad_txt)
    high_in = swap(jnp.where(first, txt_high, img_high), "core")
    low_in = swap(jnp.where(first, txt_low, img_low), "core")
    high_own = jnp.where(first, img_high, txt_high)
    low_own = jnp.where(first, img_low, txt_low)
    feats2 = jnp.concatenate([kept_feats, feats_in], axis=0)
    high2 = jnp.concatenate([high_own, high_in], axis=0)
    low2 = jnp.concatenate([low_own, low_in], axis=0)
    dims = (((0,), (0,)), ((), ()))
    part = lax.dot_general(feats2, high2, dims, preferred_element_type=f32) + lax.dot_general(
        feats2, low2, dims, preferred_element_type=f32
    )
    ds = part.shape[0]
    parts = lax.all_to_all(part.reshape(4, ds // 4, ds), "x", 0, 0, tiled=True)
    summed = parts.sum(axis=0)
    parts = lax.all_to_all(summed.reshape(8, ds // 32, ds), "z", 0, 0, tiled=True)
    summed = parts.sum(axis=0)
    other_l = swap(summed, "yl")
    other_h = swap(summed, "yh")
    other_b = lax.ppermute(summed, ("yl", "yh"), [(0, 3), (1, 2), (2, 1), (3, 0)])
    summed = (summed + other_l) + (other_h + other_b)
    spread = jnp.broadcast_to(summed[None], (8,) + summed.shape)
    gathered = lax.all_to_all(spread, "z", 0, 0, tiled=True).reshape(ds // 4, ds)
    spread = jnp.broadcast_to(gathered[None], (4,) + gathered.shape)
    own_total = lax.all_to_all(spread, "x", 0, 0, tiled=True).reshape(ds, ds)
    other_total = swap(own_total, "core")
    return (
        jnp.where(first, own_total, other_total),
        jnp.where(first, other_total, own_total),
    )


def solution(mesh):
    fine = Mesh(mesh.devices.reshape(2, 8, 4, 2, 2), AXES)
    rows = P(AXES, None)
    in_specs = (rows, P(), rows, rows, rows, P(), P(), P(AXES))
    return jax.shard_map(
        local, mesh=fine, in_specs=in_specs, out_specs=(P(), P()), check_vma=False
    )
```

```python
import jax
import jax.numpy as jnp
from jax import lax
from jax.sharding import Mesh
from jax.sharding import PartitionSpec as P

epsilon = 1e-06
scale = 20.0
shift = -1.0

AXES = ("yl", "z", "x", "core", "yh")
DP = ("yl", "z", "x", "core")
N_DP = 128

f32 = jnp.float32
bf16 = jnp.bfloat16
f16 = jnp.float16


def unit_rows(raw_rows):
    row_len = jnp.sqrt(jnp.sum(raw_rows * raw_rows, axis=1, keepdims=True) + epsilon)
    return (raw_rows / row_len, row_len)


def swap(block, axis):
    return lax.ppermute(block, axis, [(0, 1), (1, 0)])


def along_dp(block, route):
    return lax.ppermute(block, DP, route)


def chip_shift(block, step):
    return along_dp(block, [(i, (i + 2 * step) % N_DP) for i in range(N_DP)])


def pair_tile(target_rows, image_rows, row_ids, target_cols, text_cols, col_ids):
    teacher_dot = lax.dot_general(
        target_rows, target_cols, (((1,), (1,)), ((), ())), preferred_element_type=f32
    )
    labels = (row_ids[:, None] == col_ids[None, :]).astype(f32)
    target = 0.5 * jax.nn.sigmoid(scale * teacher_dot + shift) + 0.5 * labels
    logits = (
        scale
        * lax.dot_general(
            image_rows, text_cols, (((1,), (1,)), ((), ())), preferred_element_type=f32
        )
        + shift
    )
    scaled = ((jax.nn.sigmoid(logits) - target) / text_cols.shape[0]).astype(bf16)
    row_part = scale * jnp.dot(scaled, text_cols, preferred_element_type=f32)
    col_part = scale * lax.dot_general(
        scaled, image_rows, (((0,), (0,)), ((), ())), preferred_element_type=f32
    )
    return (row_part, col_part)


def direction(unit, length, grad):
    d = (grad - unit * jnp.sum(unit * grad, axis=1, keepdims=True)) / length
    high = d.astype(bf16)
    low = (d - high.astype(f32)).astype(bf16)
    return high, low


def packed(values, exponent):
    scaled = (values * jnp.exp2(-exponent)).astype(f16)
    note = jnp.full((values.shape[0], 8, values.shape[2]), exponent, f32).astype(f16)
    return jnp.concatenate([scaled, note], axis=1)


def unpacked_sum(blocks):
    exponents = blocks[:, -8, 0].astype(f32)
    scales = jnp.exp2(exponents)[:, None, None]
    return (blocks[:, :-8].astype(f32) * scales).sum(axis=0), exponents.max()


def sum_everywhere(part):
    ds = part.shape[0]
    biggest = jnp.log2(jnp.maximum(jnp.max(jnp.abs(part)), 1e-30))
    exponent = jnp.clip(jnp.ceil(biggest) - 14.0, -110.0, 110.0)
    blocks = lax.all_to_all(packed(part.reshape(4, ds // 4, ds), exponent), "x", 0, 0, tiled=True)
    summed, exponent = unpacked_sum(blocks)
    exponent = exponent + 2.0
    blocks = packed(summed.reshape(8, ds // 32, ds), exponent)
    blocks = lax.all_to_all(blocks, "z", 0, 0, tiled=True)
    summed, exponent = unpacked_sum(blocks)
    noted = jnp.concatenate([summed, jnp.full((8, ds), exponent, f32)], axis=0)
    other_l = swap(noted, "yl")
    other_h = swap(noted, "yh")
    other_b = lax.ppermute(noted, ("yl", "yh"), [(0, 3), (1, 2), (2, 1), (3, 0)])
    summed = ((noted + other_l) + (other_h + other_b))[:-8]
    exponent = jnp.maximum(exponent, jnp.maximum(other_l[-8, 0], other_h[-8, 0]))
    exponent = jnp.maximum(exponent, other_b[-8, 0]) + 5.0
    other_e = swap(jnp.full((8, 128), exponent, f32), "core")[0, 0]
    block = (summed * jnp.exp2(-exponent)).astype(f16)
    spread = jnp.broadcast_to(block[None], (8,) + block.shape)
    gathered = lax.all_to_all(spread, "z", 0, 0, tiled=True).reshape(ds // 4, ds)
    spread = jnp.broadcast_to(gathered[None], (4,) + gathered.shape)
    own_total = lax.all_to_all(spread, "x", 0, 0, tiled=True).reshape(ds, ds)
    return own_total, swap(own_total, "core"), exponent, other_e


def local(
    teacher_image,
    teacher_proj,
    teacher_text,
    image_feats,
    text_feats,
    image_proj,
    text_proj,
    class_ids,
):
    core = lax.axis_index("core")
    first = core == 0
    back_route = [(i, i - 1 if i % 2 else (i - 3) % N_DP) for i in range(N_DP)]
    step_route = [(i, (i + 1) % N_DP) for i in range(N_DP)]

    ids_y = swap(class_ids, "yh")
    ids1 = along_dp(class_ids, step_route)
    ids2 = along_dp(class_ids, [(i, (i + 2) % N_DP) for i in range(N_DP)])
    ids3 = along_dp(class_ids, [(i, (i + 3) % N_DP) for i in range(N_DP)])

    text_unit, text_len = unit_rows(jnp.dot(text_feats, text_proj, preferred_element_type=f32))
    text_emb = text_unit.astype(bf16)
    text_recv = chip_shift(text_emb, 1)
    image_unit, image_len = unit_rows(
        jnp.dot(image_feats, image_proj, preferred_element_type=f32)
    )
    image_emb = image_unit.astype(bf16)
    image_y = swap(image_emb, "yh")
    written_unit, _ = unit_rows(teacher_text.astype(f32))
    teacher_txt = written_unit.astype(bf16)
    teach_recv = chip_shift(teacher_txt, 1)
    teacher_unit, _ = unit_rows(jnp.dot(teacher_image, teacher_proj, preferred_element_type=f32))
    teacher_img = teacher_unit.astype(bf16)
    teach_y = swap(teacher_img, "yh")
    text_exch = swap(text_recv, "core")
    text_far = along_dp(jnp.where(first, text_emb, text_recv), step_route)
    teach_exch = swap(teach_recv, "core")
    teach_far = along_dp(jnp.where(first, teacher_txt, teach_recv), step_route)

    sent_feats = jnp.where(first, text_feats, image_feats)
    kept_feats = jnp.where(first, image_feats, text_feats)
    feats_in = swap(sent_feats, "core")

    image_rows = jnp.concatenate([image_emb, image_y], axis=0)
    teach_rows = jnp.concatenate([teacher_img, teach_y], axis=0)
    row_ids = jnp.concatenate([class_ids, ids_y], axis=0)
    row0, col0 = pair_tile(teach_rows, image_rows, row_ids, teacher_txt, text_emb, class_ids)
    row1, col1 = pair_tile(teach_rows, image_rows, row_ids, teach_recv, text_recv, ids2)
    ids_exch = jnp.where(first, ids1, ids3)
    row2, col2 = pair_tile(teach_rows, image_rows, row_ids, teach_exch, text_exch, ids_exch)
    both = col1 + swap(col2.astype(bf16), "core").astype(f32)
    both_back = chip_shift(both.astype(bf16), -1)
    ids_far = jnp.where(first, ids3, ids1)
    row3, col3 = pair_tile(teach_rows, image_rows, row_ids, teach_far, text_far, ids_far)
    far_back = along_dp(col3.astype(bf16), back_route)
    grad_rows = row0 + row1 + row2 + row3
    half = text_emb.shape[0]
    rows_y = swap(grad_rows[half:].astype(bf16), "yh")
    grad_img = grad_rows[:half] + rows_y.astype(f32)
    grad_txt = col0 + both_back.astype(f32) + far_back.astype(f32)

    img_high, img_low = direction(image_unit, image_len, grad_img)
    txt_high, txt_low = direction(text_unit, text_len, grad_txt)
    high_in = swap(jnp.where(first, txt_high, img_high), "core")
    low_in = swap(jnp.where(first, txt_low, img_low), "core")
    high_own = jnp.where(first, img_high, txt_high)
    low_own = jnp.where(first, img_low, txt_low)
    feats2 = jnp.concatenate([kept_feats, feats_in], axis=0)
    high2 = jnp.concatenate([high_own, high_in], axis=0)
    low2 = jnp.concatenate([low_own, low_in], axis=0)
    dims = (((0,), (0,)), ((), ()))
    part = lax.dot_general(feats2, high2, dims, preferred_element_type=f32) + lax.dot_general(
        feats2, low2, dims, preferred_element_type=f32
    )
    own_total, other_total, own_e, other_e = sum_everywhere(part)
    own_total = own_total.astype(f32) * jnp.exp2(own_e)
    other_total = other_total.astype(f32) * jnp.exp2(other_e)
    return (
        jnp.where(first, own_total, other_total),
        jnp.where(first, other_total, own_total),
    )


def solution(mesh):
    fine = Mesh(mesh.devices.reshape(2, 8, 4, 2, 2), AXES)
    rows = P(AXES, None)
    in_specs = (rows, P(), rows, rows, rows, P(), P(), P(AXES))
    return jax.shard_map(
        local, mesh=fine, in_specs=in_specs, out_specs=(P(), P()), check_vma=False
    )
```

```python
import jax
import jax.numpy as jnp
from jax import lax
from jax.sharding import Mesh
from jax.sharding import PartitionSpec as P

epsilon = 1e-06
scale = 20.0
shift = -1.0

AXES = ("yl", "z", "x", "core", "yh")
DP = ("yl", "z", "x", "core")
N_DP = 128

f32 = jnp.float32
bf16 = jnp.bfloat16
f16 = jnp.float16


def unit_rows(raw_rows):
    row_len = jnp.sqrt(jnp.sum(raw_rows * raw_rows, axis=1, keepdims=True) + epsilon)
    return (raw_rows / row_len, row_len)


def swap(block, axis):
    return lax.ppermute(block, axis, [(0, 1), (1, 0)])


def along_dp(block, route):
    return lax.ppermute(block, DP, route)


def chip_shift(block, step):
    return along_dp(block, [(i, (i + 2 * step) % N_DP) for i in range(N_DP)])


def pair_tile(teach_rows, image_rows, row_ids, teach_cols, text_cols, notes):
    teacher_dot = (
        lax.dot_general(
            teach_rows, teach_cols, (((1,), (1,)), ((), ())), preferred_element_type=f32
        )
        * notes[1:2, :]
    )
    labels = (row_ids == notes[0:1, :]).astype(f32)
    target = 0.5 * jax.nn.sigmoid(scale * teacher_dot + shift) + 0.5 * labels
    logits = (
        scale
        * lax.dot_general(
            image_rows, text_cols, (((1,), (1,)), ((), ())), preferred_element_type=f32
        )
        + shift
    )
    scaled = ((jax.nn.sigmoid(logits) - target) / text_cols.shape[0]).astype(bf16)
    row_part = scale * jnp.dot(scaled, text_cols, preferred_element_type=f32)
    col_part = scale * lax.dot_general(
        scaled, image_rows, (((0,), (0,)), ((), ())), preferred_element_type=f32
    )
    return (row_part, col_part)


def direction(unit, length, grad):
    d = (grad - unit * jnp.sum(unit * grad, axis=1, keepdims=True)) / length
    high = d.astype(bf16)
    low = (d - high.astype(f32)).astype(bf16)
    return high, low


def packed(values, exponent):
    scaled = (values * jnp.exp2(-exponent)).astype(f16)
    shape = (values.shape[0], 8, values.shape[2])
    note = jnp.broadcast_to(exponent.astype(f16), shape)
    return jnp.concatenate([scaled, note], axis=1)


def unpacked_sum(blocks):
    exponents = blocks[:, -8:-7, :].astype(f32)
    summed = (blocks[:, :-8].astype(f32) * jnp.exp2(exponents)).sum(axis=0)
    return summed, exponents.max(axis=0)


def sum_everywhere(part):
    ds = part.shape[0]
    biggest = jnp.log2(jnp.maximum(jnp.max(jnp.abs(part)), 1e-30))
    exponent = jnp.clip(jnp.ceil(biggest) - 14.0, -110.0, 110.0)
    blocks = packed(part.reshape(4, ds // 4, ds), exponent)
    blocks = lax.all_to_all(blocks, "x", 0, 0, tiled=True)
    summed, exponent = unpacked_sum(blocks)
    exponent = exponent + 2.0
    blocks = packed(summed.reshape(8, ds // 32, ds), exponent)
    blocks = lax.all_to_all(blocks, "z", 0, 0, tiled=True)
    summed, exponent = unpacked_sum(blocks)
    noted = jnp.concatenate([summed, jnp.broadcast_to(exponent, (8, ds))], axis=0)
    other_l = swap(noted, "yl")
    other_h = swap(noted, "yh")
    other_b = lax.ppermute(noted, ("yl", "yh"), [(0, 3), (1, 2), (2, 1), (3, 0)])
    summed = ((noted + other_l) + (other_h + other_b))[:-8]
    exponent = jnp.maximum(
        jnp.maximum(noted, other_l), jnp.maximum(other_h, other_b)
    )[-8:-7] + 5.0
    other_e = swap(jnp.broadcast_to(exponent, (8, ds)), "core")[0:1]
    block = (summed * jnp.exp2(-exponent)).astype(f16)
    spread = jnp.broadcast_to(block[None], (8,) + block.shape)
    gathered = lax.all_to_all(spread, "z", 0, 0, tiled=True).reshape(ds // 4, ds)
    spread = jnp.broadcast_to(gathered[None], (4,) + gathered.shape)
    own_total = lax.all_to_all(spread, "x", 0, 0, tiled=True).reshape(ds, ds)
    return own_total, swap(own_total, "core"), exponent, other_e


def local(
    teacher_image,
    teacher_proj,
    teacher_text,
    image_feats,
    text_feats,
    image_proj,
    text_proj,
    class_ids,
):
    core = lax.axis_index("core")
    first = core == 0
    back_route = [(i, i - 1 if i % 2 else (i - 3) % N_DP) for i in range(N_DP)]
    step_route = [(i, (i + 1) % N_DP) for i in range(N_DP)]

    teach_recv = chip_shift(teacher_text, 1)
    teach_y = swap(teacher_image, "yh")
    text_unit, text_len = unit_rows(jnp.dot(text_feats, text_proj, preferred_element_type=f32))
    text_emb = text_unit.astype(bf16)
    text_recv = chip_shift(text_emb, 1)
    image_first, _ = lax.optimization_barrier((image_feats, text_emb))
    image_unit, image_len = unit_rows(
        jnp.dot(image_first, image_proj, preferred_element_type=f32)
    )
    image_emb = image_unit.astype(bf16)
    image_y = swap(image_emb, "yh")
    class_ids, teacher_later, text_later, _ = lax.optimization_barrier(
        (class_ids, teacher_image, teacher_text, image_emb)
    )
    wide = text_later.astype(f32)
    inverse = 1.0 / jnp.sqrt(jnp.sum(wide * wide, axis=1) + epsilon)
    ids = class_ids.astype(f32)
    notes = jnp.stack([ids, inverse] + [ids] * 6)
    ids_y = swap(ids, "yh")
    notes_recv = chip_shift(notes, 1)
    teach_exch = swap(teach_recv, "core")
    teach_far = along_dp(jnp.where(first, teacher_text, teach_recv), step_route)
    text_exch = swap(text_recv, "core")
    text_far = along_dp(jnp.where(first, text_emb, text_recv), step_route)
    notes_exch = swap(notes_recv, "core")
    notes_far = along_dp(jnp.where(first, notes, notes_recv), step_route)

    def teacher_rows(rows):
        unit, _ = unit_rows(jnp.dot(rows, teacher_proj, preferred_element_type=f32))
        return unit.astype(bf16)

    teacher_img = teacher_rows(teacher_later)
    teacher_img_y = teacher_rows(teach_y)

    sent_feats = jnp.where(first, text_feats, image_feats)
    kept_feats = jnp.where(first, image_feats, text_feats)
    feats_in = swap(sent_feats, "core")

    image_rows = jnp.concatenate([image_emb, image_y], axis=0)
    teach_rows = jnp.concatenate([teacher_img, teacher_img_y], axis=0)
    row_ids = jnp.concatenate([ids, ids_y], axis=0)[:, None]
    rows = (teach_rows, image_rows, row_ids)
    row0, col0 = pair_tile(*rows, teacher_text, text_emb, notes)
    row1, col1 = pair_tile(*rows, teach_recv, text_recv, notes_recv)
    row2, col2 = pair_tile(*rows, teach_exch, text_exch, notes_exch)
    both = col1 + swap(col2.astype(bf16), "core").astype(f32)
    both_back = chip_shift(both.astype(bf16), -1)
    row3, col3 = pair_tile(*rows, teach_far, text_far, notes_far)
    far_back = along_dp(col3.astype(bf16), back_route)
    grad_rows = row0 + row1 + row2 + row3
    half = text_emb.shape[0]
    rows_y = swap(grad_rows[half:].astype(bf16), "yh")
    grad_img = grad_rows[:half] + rows_y.astype(f32)
    grad_txt = col0 + both_back.astype(f32) + far_back.astype(f32)

    img_high, img_low = direction(image_unit, image_len, grad_img)
    txt_high, txt_low = direction(text_unit, text_len, grad_txt)
    high_in = swap(jnp.where(first, txt_high, img_high), "core")
    low_in = swap(jnp.where(first, txt_low, img_low), "core")
    high_own = jnp.where(first, img_high, txt_high)
    low_own = jnp.where(first, img_low, txt_low)
    feats2 = jnp.concatenate([kept_feats, feats_in], axis=0)
    high2 = jnp.concatenate([high_own, high_in], axis=0)
    low2 = jnp.concatenate([low_own, low_in], axis=0)
    dims = (((0,), (0,)), ((), ()))
    part = lax.dot_general(feats2, high2, dims, preferred_element_type=f32) + lax.dot_general(
        feats2, low2, dims, preferred_element_type=f32
    )
    own_total, other_total, own_e, other_e = sum_everywhere(part)
    own_total = own_total.astype(f32) * jnp.exp2(own_e)
    other_total = other_total.astype(f32) * jnp.exp2(other_e)
    return (
        jnp.where(first, own_total, other_total),
        jnp.where(first, other_total, own_total),
    )


def solution(mesh):
    fine = Mesh(mesh.devices.reshape(2, 8, 4, 2, 2), AXES)
    rows = P(AXES, None)
    in_specs = (rows, P(), rows, rows, rows, P(), P(), P(AXES))
    return jax.shard_map(
        local, mesh=fine, in_specs=in_specs, out_specs=(P(), P()), check_vma=False
    )
```

```python
import jax
import jax.numpy as jnp
from jax import lax
from jax.sharding import Mesh
from jax.sharding import PartitionSpec as P

epsilon = 1e-06
scale = 20.0
shift = -1.0

AXES = ("yl", "z", "x", "core", "yh")
DP = ("yl", "z", "x", "core")
N_DP = 128

f32 = jnp.float32
bf16 = jnp.bfloat16
f16 = jnp.float16


def unit_rows(raw_rows):
    row_len = jnp.sqrt(jnp.sum(raw_rows * raw_rows, axis=1, keepdims=True) + epsilon)
    return (raw_rows / row_len, row_len)


def swap(block, axis):
    return lax.ppermute(block, axis, [(0, 1), (1, 0)])


def along_dp(block, route):
    return lax.ppermute(block, DP, route)


def chip_shift(block, step):
    return along_dp(block, [(i, (i + 2 * step) % N_DP) for i in range(N_DP)])


def with_ids(rows, ids):
    below = jnp.pad(ids.astype(rows.dtype)[None, :], ((0, 15), (0, rows.shape[1] - ids.shape[0])))
    return jnp.concatenate([rows, below], axis=0)


def without_ids(noted):
    count = noted.shape[0] - 16
    return noted[:count], noted[count, :count]


def pair_tile(teach_rows, image_rows, row_ids, teach_cols, noted_cols):
    text_cols, col_ids = without_ids(noted_cols)
    wide = teach_cols.astype(f32)
    inverse = 1.0 / jnp.sqrt(jnp.sum(wide * wide, axis=1) + epsilon)
    teacher_dot = (
        lax.dot_general(
            teach_rows, teach_cols, (((1,), (1,)), ((), ())), preferred_element_type=f32
        )
        * inverse[None, :]
    )
    labels = (row_ids == col_ids[None, :]).astype(f32)
    target = 0.5 * jax.nn.sigmoid(scale * teacher_dot + shift) + 0.5 * labels
    logits = (
        scale
        * lax.dot_general(
            image_rows, text_cols, (((1,), (1,)), ((), ())), preferred_element_type=f32
        )
        + shift
    )
    scaled = ((jax.nn.sigmoid(logits) - target) / text_cols.shape[0]).astype(bf16)
    row_part = scale * jnp.dot(scaled, text_cols, preferred_element_type=f32)
    col_part = scale * lax.dot_general(
        scaled, image_rows, (((0,), (0,)), ((), ())), preferred_element_type=f32
    )
    return (row_part, col_part)


def direction(unit, length, grad):
    d = (grad - unit * jnp.sum(unit * grad, axis=1, keepdims=True)) / length
    high = d.astype(bf16)
    low = (d - high.astype(f32)).astype(bf16)
    return high, low


def packed(values, exponent):
    scaled = (values * jnp.exp2(-exponent)).astype(f16)
    shape = (values.shape[0], 8, values.shape[2])
    note = jnp.broadcast_to(exponent.astype(f16), shape)
    return jnp.concatenate([scaled, note], axis=1)


def unpacked_sum(blocks):
    exponents = blocks[:, -8:-7, :].astype(f32)
    summed = (blocks[:, :-8].astype(f32) * jnp.exp2(exponents)).sum(axis=0)
    return summed, exponents.max(axis=0)


def sum_everywhere(part):
    ds = part.shape[0]
    biggest = jnp.log2(jnp.maximum(jnp.max(jnp.abs(part)), 1e-30))
    exponent = jnp.clip(jnp.ceil(biggest) - 14.0, -110.0, 110.0)
    blocks = packed(part.reshape(4, ds // 4, ds), exponent)
    blocks = lax.all_to_all(blocks, "x", 0, 0, tiled=True)
    summed, exponent = unpacked_sum(blocks)
    exponent = exponent + 2.0
    blocks = packed(summed.reshape(8, ds // 32, ds), exponent)
    blocks = lax.all_to_all(blocks, "z", 0, 0, tiled=True)
    summed, exponent = unpacked_sum(blocks)
    noted = jnp.concatenate([summed, jnp.broadcast_to(exponent, (8, ds))], axis=0)
    other_l = swap(noted, "yl")
    other_h = swap(noted, "yh")
    other_b = lax.ppermute(noted, ("yl", "yh"), [(0, 3), (1, 2), (2, 1), (3, 0)])
    summed = ((noted + other_l) + (other_h + other_b))[:-8]
    exponent = jnp.maximum(
        jnp.maximum(noted, other_l), jnp.maximum(other_h, other_b)
    )[-8:-7] + 5.0
    other_e = swap(jnp.broadcast_to(exponent, (8, ds)), "core")[0:1]
    block = (summed * jnp.exp2(-exponent)).astype(f16)
    spread = jnp.broadcast_to(block[None], (8,) + block.shape)
    gathered = lax.all_to_all(spread, "z", 0, 0, tiled=True).reshape(ds // 4, ds)
    spread = jnp.broadcast_to(gathered[None], (4,) + gathered.shape)
    own_total = lax.all_to_all(spread, "x", 0, 0, tiled=True).reshape(ds, ds)
    return own_total, swap(own_total, "core"), exponent, other_e


def local(
    teacher_image,
    teacher_proj,
    teacher_text,
    image_feats,
    text_feats,
    image_proj,
    text_proj,
    class_ids,
):
    core = lax.axis_index("core")
    first = core == 0
    back_route = [(i, i - 1 if i % 2 else (i - 3) % N_DP) for i in range(N_DP)]
    step_route = [(i, (i + 1) % N_DP) for i in range(N_DP)]

    teach_recv = chip_shift(teacher_text, 1)
    teach_y = swap(teacher_image, "yh")
    text_unit, text_len = unit_rows(jnp.dot(text_feats, text_proj, preferred_element_type=f32))
    text_own = with_ids(text_unit.astype(bf16), class_ids)
    image_first, text_own = lax.optimization_barrier((image_feats, text_own))
    text_recv = chip_shift(text_own, 1)
    image_unit, image_len = unit_rows(
        jnp.dot(image_first, image_proj, preferred_element_type=f32)
    )
    image_own = with_ids(image_unit.astype(bf16), class_ids)
    teacher_later, image_own = lax.optimization_barrier((teacher_image, image_own))
    image_y = swap(image_own, "yh")
    teach_exch = swap(teach_recv, "core")
    teach_far = along_dp(jnp.where(first, teacher_text, teach_recv), step_route)
    text_exch = swap(text_recv, "core")
    text_far = along_dp(jnp.where(first, text_own, text_recv), step_route)

    def teacher_rows(rows):
        unit, _ = unit_rows(jnp.dot(rows, teacher_proj, preferred_element_type=f32))
        return unit.astype(bf16)

    teacher_img = teacher_rows(teacher_later)
    teacher_img_y = teacher_rows(teach_y)

    sent_feats = jnp.where(first, text_feats, image_feats)
    kept_feats = jnp.where(first, image_feats, text_feats)
    feats_in = swap(sent_feats, "core")

    image_emb, ids = without_ids(image_own)
    image_emb_y, ids_y = without_ids(image_y)
    image_rows = jnp.concatenate([image_emb, image_emb_y], axis=0)
    teach_rows = jnp.concatenate([teacher_img, teacher_img_y], axis=0)
    row_ids = jnp.concatenate([ids, ids_y], axis=0)[:, None]
    rows = (teach_rows, image_rows, row_ids)
    row0, col0 = pair_tile(*rows, teacher_text, text_own)
    row1, col1 = pair_tile(*rows, teach_recv, text_recv)
    row2, col2 = pair_tile(*rows, teach_exch, text_exch)
    both = col1 + swap(col2.astype(bf16), "core").astype(f32)
    both_back = chip_shift(both.astype(bf16), -1)
    row3, col3 = pair_tile(*rows, teach_far, text_far)
    far_back = along_dp(col3.astype(bf16), back_route)
    grad_rows = row0 + row1 + row2 + row3
    half = image_emb.shape[0]
    rows_y = swap(grad_rows[half:].astype(bf16), "yh")
    grad_img = grad_rows[:half] + rows_y.astype(f32)
    grad_txt = col0 + both_back.astype(f32) + far_back.astype(f32)

    img_high, img_low = direction(image_unit, image_len, grad_img)
    txt_high, txt_low = direction(text_unit, text_len, grad_txt)
    high_in = swap(jnp.where(first, txt_high, img_high), "core")
    low_in = swap(jnp.where(first, txt_low, img_low), "core")
    high_own = jnp.where(first, img_high, txt_high)
    low_own = jnp.where(first, img_low, txt_low)
    feats2 = jnp.concatenate([kept_feats, feats_in], axis=0)
    high2 = jnp.concatenate([high_own, high_in], axis=0)
    low2 = jnp.concatenate([low_own, low_in], axis=0)
    dims = (((0,), (0,)), ((), ()))
    part = lax.dot_general(feats2, high2, dims, preferred_element_type=f32) + lax.dot_general(
        feats2, low2, dims, preferred_element_type=f32
    )
    own_total, other_total, own_e, other_e = sum_everywhere(part)
    own_total = own_total.astype(f32) * jnp.exp2(own_e)
    other_total = other_total.astype(f32) * jnp.exp2(other_e)
    return (
        jnp.where(first, own_total, other_total),
        jnp.where(first, other_total, own_total),
    )


def solution(mesh):
    fine = Mesh(mesh.devices.reshape(2, 8, 4, 2, 2), AXES)
    rows = P(AXES, None)
    in_specs = (rows, P(), rows, rows, rows, P(), P(), P(AXES))
    return jax.shard_map(
        local, mesh=fine, in_specs=in_specs, out_specs=(P(), P()), check_vma=False
    )
```

```python
import jax
import jax.numpy as jnp
from jax import lax
from jax.experimental import pallas as pl
from jax.experimental.pallas import tpu as pltpu
from jax.sharding import Mesh
from jax.sharding import PartitionSpec as P

epsilon = 1e-06
scale = 20.0
shift = -1.0

AXES = ("yl", "z", "x", "core", "yh")
DP = ("yl", "z", "x", "core")
N_DP = 128
COST1 = 10**10
COST2 = 2 * 10**10

f32 = jnp.float32
bf16 = jnp.bfloat16
f16 = jnp.float16


def unit_rows(raw_rows):
    row_len = jnp.sqrt(jnp.sum(raw_rows * raw_rows, axis=1, keepdims=True) + epsilon)
    return (raw_rows / row_len, row_len)


def swap(block, axis):
    return lax.ppermute(block, axis, [(0, 1), (1, 0)])


def along_dp(block, route):
    return lax.ppermute(block, DP, route)


def chip_shift(block, step):
    return along_dp(block, [(i, (i + 2 * step) % N_DP) for i in range(N_DP)])


def forward(block):
    direct = along_dp(block, [(i, (i + 2) % N_DP) for i in range(N_DP) if i not in (62, 126)])
    aside = along_dp(block, [(126, 56), (62, 120)])
    aside = along_dp(aside, [(56, 0), (120, 64)])
    return direct, aside


def hand_on_kernel(flag, own, got, onward):
    onward[...] = jnp.where(flag[0] == 1, own[...], got[...])


def hand_on(first, own, got, flops):
    block = pl.BlockSpec((own.shape[0] // 2, own.shape[1]), lambda i, flag: (i, 0))
    return pl.pallas_call(
        hand_on_kernel,
        grid_spec=pltpu.PrefetchScalarGridSpec(
            num_scalar_prefetch=1, grid=(2,), in_specs=[block] * 2, out_specs=block
        ),
        out_shape=jax.ShapeDtypeStruct(own.shape, own.dtype),
        cost_estimate=pl.CostEstimate(flops=flops, bytes_accessed=own.size * 6, transcendentals=0),
    )(first.astype(jnp.int32)[None], own, got)


def with_ids(rows, ids):
    below = jnp.pad(ids.astype(rows.dtype)[None, :], ((0, 15), (0, rows.shape[1] - ids.shape[0])))
    return jnp.concatenate([rows, below], axis=0)


def without_ids(noted):
    count = noted.shape[0] - 16
    return noted[:count], noted[count, :count]


def pair_tile(teach_rows, image_rows, row_ids, teach_cols, noted_cols):
    text_cols, col_ids = without_ids(noted_cols)
    wide = teach_cols.astype(f32)
    inverse = 1.0 / jnp.sqrt(jnp.sum(wide * wide, axis=1) + epsilon)
    teacher_dot = (
        lax.dot_general(
            teach_rows, teach_cols, (((1,), (1,)), ((), ())), preferred_element_type=f32
        )
        * inverse[None, :]
    )
    labels = (row_ids == col_ids[None, :]).astype(f32)
    target = 0.5 * jax.nn.sigmoid(scale * teacher_dot + shift) + 0.5 * labels
    logits = (
        scale
        * lax.dot_general(
            image_rows, text_cols, (((1,), (1,)), ((), ())), preferred_element_type=f32
        )
        + shift
    )
    scaled = ((jax.nn.sigmoid(logits) - target) / text_cols.shape[0]).astype(bf16)
    row_part = scale * jnp.dot(scaled, text_cols, preferred_element_type=f32)
    col_part = scale * lax.dot_general(
        scaled, image_rows, (((0,), (0,)), ((), ())), preferred_element_type=f32
    )
    return (row_part, col_part)


def direction(unit, length, grad):
    d = (grad - unit * jnp.sum(unit * grad, axis=1, keepdims=True)) / length
    high = d.astype(bf16)
    low = (d - high.astype(f32)).astype(bf16)
    return high, low


def packed(values, exponent):
    scaled = (values * jnp.exp2(-exponent)).astype(f16)
    shape = (values.shape[0], 8, values.shape[2])
    note = jnp.broadcast_to(exponent.astype(f16), shape)
    return jnp.concatenate([scaled, note], axis=1)


def unpacked_sum(blocks):
    exponents = blocks[:, -8:-7, :].astype(f32)
    summed = (blocks[:, :-8].astype(f32) * jnp.exp2(exponents)).sum(axis=0)
    return summed, exponents.max(axis=0)


def sum_everywhere(part):
    ds = part.shape[0]
    biggest = jnp.log2(jnp.maximum(jnp.max(jnp.abs(part)), 1e-30))
    exponent = jnp.clip(jnp.ceil(biggest) - 14.0, -110.0, 110.0)
    blocks = packed(part.reshape(4, ds // 4, ds), exponent)
    blocks = lax.all_to_all(blocks, "x", 0, 0, tiled=True)
    summed, exponent = unpacked_sum(blocks)
    exponent = exponent + 2.0
    blocks = packed(summed.reshape(8, ds // 32, ds), exponent)
    blocks = lax.all_to_all(blocks, "z", 0, 0, tiled=True)
    summed, exponent = unpacked_sum(blocks)
    noted = jnp.concatenate([summed, jnp.broadcast_to(exponent, (8, ds))], axis=0)
    other_l = swap(noted, "yl")
    other_h = swap(noted, "yh")
    other_b = lax.ppermute(noted, ("yl", "yh"), [(0, 3), (1, 2), (2, 1), (3, 0)])
    summed = ((noted + other_l) + (other_h + other_b))[:-8]
    exponent = jnp.maximum(
        jnp.maximum(noted, other_l), jnp.maximum(other_h, other_b)
    )[-8:-7] + 5.0
    other_e = swap(jnp.broadcast_to(exponent, (8, ds)), "core")[0:1]
    block = (summed * jnp.exp2(-exponent)).astype(f16)
    spread = jnp.broadcast_to(block[None], (8,) + block.shape)
    gathered = lax.all_to_all(spread, "z", 0, 0, tiled=True).reshape(ds // 4, ds)
    spread = jnp.broadcast_to(gathered[None], (4,) + gathered.shape)
    own_total = lax.all_to_all(spread, "x", 0, 0, tiled=True).reshape(ds, ds)
    return own_total, swap(own_total, "core"), exponent, other_e


def local(
    teacher_image,
    teacher_proj,
    teacher_text,
    image_feats,
    text_feats,
    image_proj,
    text_proj,
    class_ids,
):
    core = lax.axis_index("core")
    first = core == 0
    back_route = [(i, i - 1 if i % 2 else (i - 3) % N_DP) for i in range(N_DP)]
    step_route = [(i, (i + 1) % N_DP) for i in range(N_DP)]

    teach_direct, teach_aside = forward(teacher_text)
    teach_y = swap(teacher_image, "yh")
    text_unit, text_len = unit_rows(jnp.dot(text_feats, text_proj, preferred_element_type=f32))
    text_own = with_ids(text_unit.astype(bf16), class_ids)
    image_first, text_own = lax.optimization_barrier((image_feats, text_own))
    text_recv = chip_shift(text_own, 1)
    image_unit, image_len = unit_rows(
        jnp.dot(image_first, image_proj, preferred_element_type=f32)
    )
    image_own = with_ids(image_unit.astype(bf16), class_ids)
    teacher_later, image_own = lax.optimization_barrier((teacher_image, image_own))
    image_y = swap(image_own, "yh")
    teach_far = along_dp(hand_on(first, teacher_text, teach_direct, COST2), step_route)
    text_far = along_dp(hand_on(first, text_own, text_recv, COST1), step_route)
    crossed = lax.axis_index(DP) % 64 == 0
    teach_recv = jnp.where(crossed, teach_aside, teach_direct)
    text_exch = swap(text_recv, "core")
    teach_exch = swap(teach_recv, "core")

    def teacher_rows(rows):
        unit, _ = unit_rows(jnp.dot(rows, teacher_proj, preferred_element_type=f32))
        return unit.astype(bf16)

    teacher_img = teacher_rows(teacher_later)
    teacher_img_y = teacher_rows(teach_y)

    sent_feats = jnp.where(first, text_feats, image_feats)
    kept_feats = jnp.where(first, image_feats, text_feats)
    feats_in = swap(sent_feats, "core")

    image_emb, ids = without_ids(image_own)
    image_emb_y, ids_y = without_ids(image_y)
    image_rows = jnp.concatenate([image_emb, image_emb_y], axis=0)
    teach_rows = jnp.concatenate([teacher_img, teacher_img_y], axis=0)
    row_ids = jnp.concatenate([ids, ids_y], axis=0)[:, None]
    rows = (teach_rows, image_rows, row_ids)
    row0, col0 = pair_tile(*rows, teacher_text, text_own)
    row1, col1 = pair_tile(*rows, teach_recv, text_recv)
    row2, col2 = pair_tile(*rows, teach_exch, text_exch)
    both = col1 + swap(col2.astype(bf16), "core").astype(f32)
    both_back = chip_shift(both.astype(bf16), -1)
    row3, col3 = pair_tile(*rows, teach_far, text_far)
    far_back = along_dp(col3.astype(bf16), back_route)
    grad_rows = row0 + row1 + row2 + row3
    half = image_emb.shape[0]
    rows_y = swap(grad_rows[half:].astype(bf16), "yh")
    grad_img = grad_rows[:half] + rows_y.astype(f32)
    grad_txt = col0 + both_back.astype(f32) + far_back.astype(f32)

    img_high, img_low = direction(image_unit, image_len, grad_img)
    txt_high, txt_low = direction(text_unit, text_len, grad_txt)
    high_in = swap(jnp.where(first, txt_high, img_high), "core")
    low_in = swap(jnp.where(first, txt_low, img_low), "core")
    high_own = jnp.where(first, img_high, txt_high)
    low_own = jnp.where(first, img_low, txt_low)
    feats2 = jnp.concatenate([kept_feats, feats_in], axis=0)
    high2 = jnp.concatenate([high_own, high_in], axis=0)
    low2 = jnp.concatenate([low_own, low_in], axis=0)
    dims = (((0,), (0,)), ((), ()))
    part = lax.dot_general(feats2, high2, dims, preferred_element_type=f32) + lax.dot_general(
        feats2, low2, dims, preferred_element_type=f32
    )
    own_total, other_total, own_e, other_e = sum_everywhere(part)
    own_total = own_total.astype(f32) * jnp.exp2(own_e)
    other_total = other_total.astype(f32) * jnp.exp2(other_e)
    return (
        jnp.where(first, own_total, other_total),
        jnp.where(first, other_total, own_total),
    )


def solution(mesh):
    fine = Mesh(mesh.devices.reshape(2, 8, 4, 2, 2), AXES)
    rows = P(AXES, None)
    in_specs = (rows, P(), rows, rows, rows, P(), P(), P(AXES))
    return jax.shard_map(
        local, mesh=fine, in_specs=in_specs, out_specs=(P(), P()), check_vma=False
    )
```

```python
import jax
import jax.numpy as jnp
from jax import lax
from jax.experimental import pallas as pl
from jax.experimental.pallas import tpu as pltpu
from jax.sharding import Mesh
from jax.sharding import PartitionSpec as P

epsilon = 1e-06
scale = 20.0
shift = -1.0

AXES = ("yl", "z", "x", "core", "yh")
DP = ("yl", "z", "x", "core")
N_DP = 128

f32 = jnp.float32
bf16 = jnp.bfloat16
f16 = jnp.float16


def unit_rows(raw_rows):
    row_len = jnp.sqrt(jnp.sum(raw_rows * raw_rows, axis=1, keepdims=True) + epsilon)
    return (raw_rows / row_len, row_len)


def swap(block, axis):
    return lax.ppermute(block, axis, [(0, 1), (1, 0)])


def along_dp(block, route):
    return lax.ppermute(block, DP, route)


def chip_shift(block, step):
    return along_dp(block, [(i, (i + 2 * step) % N_DP) for i in range(N_DP)])


VMEM = pl.BlockSpec(memory_space=pltpu.VMEM)
SMEM = pl.BlockSpec(memory_space=pltpu.SMEM)
ROWS = 256
DT = 1536
DS = 768
PAD = 16


def note_ids(ids, payload):
    payload[ROWS:, :] = jnp.zeros((PAD, DT + DS), bf16)
    payload[ROWS:, :ROWS] = jnp.broadcast_to(ids[...], (PAD, ROWS)).astype(f32).astype(bf16)


def student(feats, proj, payload, unit_out, len_out):
    unit, length = unit_rows(jnp.dot(feats[...], proj[...], preferred_element_type=f32))
    payload[:ROWS, DT:] = unit.astype(bf16)
    unit_out[...] = unit
    len_out[...] = length


def text_kernel(ids, feats, proj, teacher, payload, unit_out, len_out):
    student(feats, proj, payload, unit_out, len_out)
    unit, _ = unit_rows(teacher[...].astype(f32))
    payload[:ROWS, :DT] = unit.astype(bf16)
    note_ids(ids, payload)


def image_kernel(ids, feats, proj, teacher, teacher_proj, payload, unit_out, len_out):
    student(feats, proj, payload, unit_out, len_out)
    unit, _ = unit_rows(jnp.dot(teacher[...], teacher_proj[...], preferred_element_type=f32))
    payload[:ROWS, :DT] = unit.astype(bf16)
    note_ids(ids, payload)


def embed(kernel, flops, *args):
    return pl.pallas_call(
        kernel,
        in_specs=[VMEM] * len(args),
        out_specs=[VMEM] * 3,
        out_shape=[
            jax.ShapeDtypeStruct((ROWS + PAD, DT + DS), bf16),
            jax.ShapeDtypeStruct((ROWS, DS), f32),
            jax.ShapeDtypeStruct((ROWS, 1), f32),
        ],
        compiler_params=pltpu.CompilerParams(vmem_limit_bytes=48 * 2**20),
        cost_estimate=pl.CostEstimate(flops=flops, bytes_accessed=5 * 2**20, transcendentals=0),
    )(*args)


CROSS = (((1,), (1,)), ((), ()))
OVER_ROWS = (((0,), (0,)), ((), ()))


def tile(image, text):
    teacher_dot = lax.dot_general(
        image[:ROWS, :DT], text[:ROWS, :DT], CROSS, preferred_element_type=f32
    )
    row_ids = jnp.broadcast_to(image[ROWS:, :ROWS].astype(f32)[:1], (ROWS, ROWS)).T
    labels = (row_ids == text[ROWS:, :ROWS].astype(f32)[:1]).astype(f32)
    target = 0.5 * jax.nn.sigmoid(scale * teacher_dot + shift) + 0.5 * labels
    logits = (
        scale
        * lax.dot_general(
            image[:ROWS, DT:], text[:ROWS, DT:], CROSS, preferred_element_type=f32
        )
        + shift
    )
    resid = ((jax.nn.sigmoid(logits) - target) * (1.0 / ROWS)).astype(bf16)
    row_part = scale * jnp.dot(resid, text[:ROWS, DT:], preferred_element_type=f32)
    col_part = scale * lax.dot_general(
        resid, image[:ROWS, DT:], OVER_ROWS, preferred_element_type=f32
    )
    return row_part, col_part


def near_kernel(own, other, text, recv, rows, col0, col1):
    row_a, col_a = tile(own, text)
    row_b, col_b = tile(own, recv)
    rows[:ROWS] = row_a + row_b
    row_a, col_c = tile(other, text)
    row_b, col_d = tile(other, recv)
    rows[ROWS:] = row_a + row_b
    col0[...] = col_a + col_c
    col1[...] = col_b + col_d


def exch_kernel(own, other, text, rows, col):
    row_a, col_a = tile(own, text)
    rows[:ROWS] = row_a
    row_b, col_b = tile(other, text)
    rows[ROWS:] = row_b
    col[...] = (col_a + col_b).astype(bf16)


def far_kernel(flag, own, other, beside, behind, rows, more_rows, own_rows, other_rows, col, text):
    text[...] = jnp.where(flag[0] == 1, behind[...], beside[...])
    row_a, col_a = tile(own, text)
    row_b, col_b = tile(other, text)
    col[...] = (col_a + col_b).astype(bf16)
    own_rows[...] = row_a + rows[:ROWS] + more_rows[:ROWS]
    other_rows[...] = (row_b + rows[ROWS:] + more_rows[ROWS:]).astype(bf16)


def pairs(kernel, specs, outs, scratch, tiles, *args):
    return pl.pallas_call(
        kernel,
        in_specs=specs,
        out_specs=[VMEM] * len(outs),
        out_shape=[jax.ShapeDtypeStruct(shape, dtype) for shape, dtype in outs],
        scratch_shapes=scratch,
        compiler_params=pltpu.CompilerParams(vmem_limit_bytes=48 * 2**20),
        cost_estimate=pl.CostEstimate(
            flops=tiles * 10**9, bytes_accessed=tiles * 3 * 2**20, transcendentals=0
        ),
    )(*args)


def direction(unit, length, grad):
    d = (grad - unit * jnp.sum(unit * grad, axis=1, keepdims=True)) / length
    high = d.astype(bf16)
    low = (d - high.astype(f32)).astype(bf16)
    return high, low


def packed(values, exponent):
    scaled = (values * jnp.exp2(-exponent)).astype(f16)
    shape = (values.shape[0], 8, values.shape[2])
    note = jnp.broadcast_to(exponent.astype(f16), shape)
    return jnp.concatenate([scaled, note], axis=1)


def unpacked_sum(blocks):
    exponents = blocks[:, -8:-7, :].astype(f32)
    summed = (blocks[:, :-8].astype(f32) * jnp.exp2(exponents)).sum(axis=0)
    return summed, exponents.max(axis=0)


def sum_everywhere(part):
    ds = part.shape[0]
    biggest = jnp.log2(jnp.maximum(jnp.max(jnp.abs(part)), 1e-30))
    exponent = jnp.clip(jnp.ceil(biggest) - 14.0, -110.0, 110.0)
    blocks = packed(part.reshape(4, ds // 4, ds), exponent)
    blocks = lax.all_to_all(blocks, "x", 0, 0, tiled=True)
    summed, exponent = unpacked_sum(blocks)
    exponent = exponent + 2.0
    blocks = packed(summed.reshape(8, ds // 32, ds), exponent)
    blocks = lax.all_to_all(blocks, "z", 0, 0, tiled=True)
    summed, exponent = unpacked_sum(blocks)
    noted = jnp.concatenate([summed, jnp.broadcast_to(exponent, (8, ds))], axis=0)
    other_l = swap(noted, "yl")
    other_h = swap(noted, "yh")
    other_b = lax.ppermute(noted, ("yl", "yh"), [(0, 3), (1, 2), (2, 1), (3, 0)])
    summed = ((noted + other_l) + (other_h + other_b))[:-8]
    exponent = jnp.maximum(
        jnp.maximum(noted, other_l), jnp.maximum(other_h, other_b)
    )[-8:-7] + 5.0
    other_e = swap(jnp.broadcast_to(exponent, (8, ds)), "core")[0:1]
    block = (summed * jnp.exp2(-exponent)).astype(f16)
    spread = jnp.broadcast_to(block[None], (8,) + block.shape)
    gathered = lax.all_to_all(spread, "z", 0, 0, tiled=True).reshape(ds // 4, ds)
    spread = jnp.broadcast_to(gathered[None], (4,) + gathered.shape)
    own_total = lax.all_to_all(spread, "x", 0, 0, tiled=True).reshape(ds, ds)
    return own_total, swap(own_total, "core"), exponent, other_e


def local(
    teacher_image,
    teacher_proj,
    teacher_text,
    image_feats,
    text_feats,
    image_proj,
    text_proj,
    class_ids,
):
    core = lax.axis_index("core")
    first = core == 0
    back_route = [(i, i - 1 if i % 2 else (i - 3) % N_DP) for i in range(N_DP)]
    ids = class_ids[None, :]
    text_own, text_unit, text_len = embed(
        text_kernel, 10**9, ids, text_feats, text_proj, teacher_text
    )
    ids, image_feats, teacher_image, text_own = lax.optimization_barrier(
        (ids, image_feats, teacher_image, text_own)
    )
    recv = chip_shift(text_own, 1)
    beside = along_dp(text_own, [(i, i + 1) for i in range(0, N_DP, 2)])
    image_own, image_unit, image_len = embed(
        image_kernel, 2 * 10**9, ids, image_feats, image_proj, teacher_image, teacher_proj
    )
    image_y = swap(image_own, "yh")
    behind = along_dp(recv, [(i, (i + 1) % N_DP) for i in range(1, N_DP, 2)])
    exch = swap(recv, "core")

    sent_feats = jnp.where(first, text_feats, image_feats)
    kept_feats = jnp.where(first, image_feats, text_feats)
    feats_in = swap(sent_feats, "core")

    wide, narrow = ((2 * ROWS, DS), f32), ((ROWS, DS), bf16)
    block = ((ROWS, DS), f32)
    rows, col0, col1 = pairs(
        near_kernel, [VMEM] * 4, [wide, block, block], [], 4, image_own, image_y, text_own, recv
    )
    more_rows, col2 = pairs(
        exch_kernel, [VMEM] * 3, [wide, narrow], [], 2, image_own, image_y, exch
    )
    both = (col1 + swap(col2, "core").astype(f32)).astype(bf16)
    both, behind = lax.optimization_barrier((both, behind))
    both_back = chip_shift(both, -1)
    own_rows, other_rows, col3 = pairs(
        far_kernel,
        [SMEM] + [VMEM] * 6,
        [block, narrow, narrow],
        [pltpu.VMEM((ROWS + PAD, DT + DS), bf16)],
        2,
        first.astype(jnp.int32)[None],
        image_own,
        image_y,
        beside,
        behind,
        rows,
        more_rows,
    )
    far_back = along_dp(col3, back_route)
    rows_y = swap(other_rows, "yh")
    grad_img = own_rows + rows_y.astype(f32)
    grad_txt = col0 + both_back.astype(f32) + far_back.astype(f32)

    img_high, img_low = direction(image_unit, image_len, grad_img)
    txt_high, txt_low = direction(text_unit, text_len, grad_txt)
    high_in = swap(jnp.where(first, txt_high, img_high), "core")
    low_in = swap(jnp.where(first, txt_low, img_low), "core")
    high_own = jnp.where(first, img_high, txt_high)
    low_own = jnp.where(first, img_low, txt_low)
    feats2 = jnp.concatenate([kept_feats, feats_in], axis=0)
    high2 = jnp.concatenate([high_own, high_in], axis=0)
    low2 = jnp.concatenate([low_own, low_in], axis=0)
    dims = (((0,), (0,)), ((), ()))
    part = lax.dot_general(feats2, high2, dims, preferred_element_type=f32) + lax.dot_general(
        feats2, low2, dims, preferred_element_type=f32
    )
    own_total, other_total, own_e, other_e = sum_everywhere(part)
    own_total = own_total.astype(f32) * jnp.exp2(own_e)
    other_total = other_total.astype(f32) * jnp.exp2(other_e)
    return (
        jnp.where(first, own_total, other_total),
        jnp.where(first, other_total, own_total),
    )


def solution(mesh):
    fine = Mesh(mesh.devices.reshape(2, 8, 4, 2, 2), AXES)
    rows = P(AXES, None)
    in_specs = (rows, P(), rows, rows, rows, P(), P(), P(AXES))
    return jax.shard_map(
        local, mesh=fine, in_specs=in_specs, out_specs=(P(), P()), check_vma=False
    )
```

```python
import jax
import jax.numpy as jnp
from jax import lax
from jax.experimental import pallas as pl
from jax.experimental.pallas import tpu as pltpu
from jax.sharding import Mesh
from jax.sharding import PartitionSpec as P

epsilon = 1e-06
scale = 20.0
shift = -1.0

AXES = ("yl", "z", "x", "core", "yh")
DP = ("yl", "z", "x", "core")
N_DP = 128

f32 = jnp.float32
bf16 = jnp.bfloat16
f16 = jnp.float16


def unit_rows(raw_rows):
    row_len = jnp.sqrt(jnp.sum(raw_rows * raw_rows, axis=1, keepdims=True) + epsilon)
    return (raw_rows / row_len, row_len)


def swap(block, axis):
    return lax.ppermute(block, axis, [(0, 1), (1, 0)])


def along_dp(block, route):
    return lax.ppermute(block, DP, route)


def chip_shift(block, step):
    return along_dp(block, [(i, (i + 2 * step) % N_DP) for i in range(N_DP)])


def forward(block):
    direct = along_dp(block, [(i, (i + 2) % N_DP) for i in range(N_DP) if i not in (62, 126)])
    aside = along_dp(block, [(126, 56), (62, 120)])
    return direct, aside


VMEM = pl.BlockSpec(memory_space=pltpu.VMEM)
SMEM = pl.BlockSpec(memory_space=pltpu.SMEM)
ROWS = 256
DT = 1536
DS = 768
PAD = 16
FAR_COST = 40
OWN_COST = 2


def note_ids(ids, payload):
    payload[ROWS:, :] = jnp.zeros((PAD, DT + DS), bf16)
    payload[ROWS:, :ROWS] = jnp.broadcast_to(ids[...], (PAD, ROWS)).astype(f32).astype(bf16)


def student(feats, proj, payload, unit_out, len_out):
    unit, length = unit_rows(jnp.dot(feats[...], proj[...], preferred_element_type=f32))
    payload[:ROWS, DT:] = unit.astype(bf16)
    unit_out[...] = unit
    len_out[...] = length


def text_kernel(ids, feats, proj, teacher, payload, unit_out, len_out):
    student(feats, proj, payload, unit_out, len_out)
    unit, _ = unit_rows(teacher[...].astype(f32))
    payload[:ROWS, :DT] = unit.astype(bf16)
    note_ids(ids, payload)


def image_kernel(ids, feats, proj, teacher, teacher_proj, payload, unit_out, len_out):
    student(feats, proj, payload, unit_out, len_out)
    unit, _ = unit_rows(jnp.dot(teacher[...], teacher_proj[...], preferred_element_type=f32))
    payload[:ROWS, :DT] = unit.astype(bf16)
    note_ids(ids, payload)


def embed(kernel, flops, *args):
    return pl.pallas_call(
        kernel,
        in_specs=[VMEM] * len(args),
        out_specs=[VMEM] * 3,
        out_shape=[
            jax.ShapeDtypeStruct((ROWS + PAD, DT + DS), bf16),
            jax.ShapeDtypeStruct((ROWS, DS), f32),
            jax.ShapeDtypeStruct((ROWS, 1), f32),
        ],
        compiler_params=pltpu.CompilerParams(vmem_limit_bytes=28 * 2**20),
        cost_estimate=pl.CostEstimate(flops=flops, bytes_accessed=5 * 2**20, transcendentals=0),
    )(*args)


CROSS = (((1,), (1,)), ((), ()))
OVER_ROWS = (((0,), (0,)), ((), ()))


def tile(image, text):
    teacher_dot = lax.dot_general(
        image[:ROWS, :DT], text[:ROWS, :DT], CROSS, preferred_element_type=f32
    )
    row_ids = jnp.broadcast_to(image[ROWS:, :ROWS].astype(f32)[:1], (ROWS, ROWS)).T
    labels = (row_ids == text[ROWS:, :ROWS].astype(f32)[:1]).astype(f32)
    target = 0.5 * jax.nn.sigmoid(scale * teacher_dot + shift) + 0.5 * labels
    logits = (
        scale
        * lax.dot_general(
            image[:ROWS, DT:], text[:ROWS, DT:], CROSS, preferred_element_type=f32
        )
        + shift
    )
    resid = ((jax.nn.sigmoid(logits) - target) * (1.0 / ROWS)).astype(bf16)
    row_part = scale * jnp.dot(resid, text[:ROWS, DT:], preferred_element_type=f32)
    col_part = scale * lax.dot_general(
        resid, image[:ROWS, DT:], OVER_ROWS, preferred_element_type=f32
    )
    return row_part, col_part


def own_kernel(own, other, text, rows, col):
    row_a, col_a = tile(own, text)
    rows[:ROWS] = row_a
    row_b, col_b = tile(other, text)
    rows[ROWS:] = row_b
    col[...] = col_a + col_b


def near_kernel(
    flags, own, other, direct, aside, exch, aside_exch, before, rows, col1, col2, recv, swapped
):
    recv[...] = jnp.where(flags[0] == 1, aside[...], direct[...])
    swapped[...] = jnp.where(flags[1] == 1, aside_exch[...], exch[...])
    row_a, col_a = tile(own, swapped)
    row_b, col_b = tile(own, recv)
    rows[:ROWS] = row_a + row_b + before[:ROWS]
    row_a, col_c = tile(other, swapped)
    row_b, col_d = tile(other, recv)
    rows[ROWS:] = row_a + row_b + before[ROWS:]
    col2[...] = (col_a + col_c).astype(bf16)
    col1[...] = col_b + col_d


def far_kernel(flag, own, other, beside, behind, rows, own_rows, other_rows, col, text):
    text[...] = jnp.where(flag[0] == 1, behind[...], beside[...])
    row_a, col_a = tile(own, text)
    row_b, col_b = tile(other, text)
    col[...] = (col_a + col_b).astype(bf16)
    own_rows[...] = row_a + rows[:ROWS]
    other_rows[...] = (row_b + rows[ROWS:]).astype(bf16)


def pairs(kernel, specs, outs, scratch, tiles, *args):
    return pl.pallas_call(
        kernel,
        in_specs=specs,
        out_specs=[VMEM] * len(outs),
        out_shape=[jax.ShapeDtypeStruct(shape, dtype) for shape, dtype in outs],
        scratch_shapes=scratch,
        compiler_params=pltpu.CompilerParams(vmem_limit_bytes=28 * 2**20),
        cost_estimate=pl.CostEstimate(
            flops=tiles * 10**9, bytes_accessed=tiles * 3 * 2**20, transcendentals=0
        ),
    )(*args)


def direction(unit, length, grad):
    d = (grad - unit * jnp.sum(unit * grad, axis=1, keepdims=True)) / length
    high = d.astype(bf16)
    low = (d - high.astype(f32)).astype(bf16)
    return high, low


def packed(values, exponent):
    scaled = (values * jnp.exp2(-exponent)).astype(f16)
    shape = (values.shape[0], 8, values.shape[2])
    note = jnp.broadcast_to(exponent.astype(f16), shape)
    return jnp.concatenate([scaled, note], axis=1)


def unpacked_sum(blocks):
    exponents = blocks[:, -8:-7, :].astype(f32)
    summed = (blocks[:, :-8].astype(f32) * jnp.exp2(exponents)).sum(axis=0)
    return summed, exponents.max(axis=0)


def sum_everywhere(part):
    ds = part.shape[0]
    biggest = jnp.log2(jnp.maximum(jnp.max(jnp.abs(part)), 1e-30))
    exponent = jnp.clip(jnp.ceil(biggest) - 14.0, -110.0, 110.0)
    blocks = packed(part.reshape(4, ds // 4, ds), exponent)
    blocks = lax.all_to_all(blocks, "x", 0, 0, tiled=True)
    summed, exponent = unpacked_sum(blocks)
    exponent = exponent + 2.0
    blocks = packed(summed.reshape(8, ds // 32, ds), exponent)
    blocks = lax.all_to_all(blocks, "z", 0, 0, tiled=True)
    summed, exponent = unpacked_sum(blocks)
    noted = jnp.concatenate([summed, jnp.broadcast_to(exponent, (8, ds))], axis=0)
    other_l = swap(noted, "yl")
    other_h = swap(noted, "yh")
    other_b = lax.ppermute(noted, ("yl", "yh"), [(0, 3), (1, 2), (2, 1), (3, 0)])
    summed = ((noted + other_l) + (other_h + other_b))[:-8]
    exponent = jnp.maximum(
        jnp.maximum(noted, other_l), jnp.maximum(other_h, other_b)
    )[-8:-7] + 5.0
    other_e = swap(jnp.broadcast_to(exponent, (8, ds)), "core")[0:1]
    block = (summed * jnp.exp2(-exponent)).astype(f16)
    spread = jnp.broadcast_to(block[None], (8,) + block.shape)
    gathered = lax.all_to_all(spread, "z", 0, 0, tiled=True).reshape(ds // 4, ds)
    spread = jnp.broadcast_to(gathered[None], (4,) + gathered.shape)
    own_total = lax.all_to_all(spread, "x", 0, 0, tiled=True).reshape(ds, ds)
    return own_total, swap(own_total, "core"), exponent, other_e


def local(
    teacher_image,
    teacher_proj,
    teacher_text,
    image_feats,
    text_feats,
    image_proj,
    text_proj,
    class_ids,
):
    core = lax.axis_index("core")
    first = core == 0
    back_route = [(i, i - 1 if i % 2 else (i - 3) % N_DP) for i in range(N_DP)]
    ids = class_ids[None, :]
    text_own, text_unit, text_len = embed(
        text_kernel, 10**9, ids, text_feats, text_proj, teacher_text
    )
    ids, image_feats, teacher_image, text_own = lax.optimization_barrier(
        (ids, image_feats, teacher_image, text_own)
    )
    recv, aside = forward(text_own)
    beside = along_dp(text_own, [(i, i + 1) for i in range(0, N_DP, 2)])
    image_own, image_unit, image_len = embed(
        image_kernel, 2 * 10**9, ids, image_feats, image_proj, teacher_image, teacher_proj
    )
    image_y = swap(image_own, "yh")
    recv, aside, beside, image_later = lax.optimization_barrier((recv, aside, beside, image_own))
    aside_exch = along_dp(aside, [(56, 1), (120, 65)])
    aside = along_dp(aside, [(56, 0), (120, 64)])
    behind = along_dp(recv, [(i, (i + 1) % N_DP) for i in range(1, N_DP, 2)])
    exch = along_dp(recv, [(i, i ^ 1) for i in range(N_DP) if i not in (0, 64)])

    sent_feats = jnp.where(first, text_feats, image_feats)
    kept_feats = jnp.where(first, image_feats, text_feats)
    feats_in = swap(sent_feats, "core")

    wide, narrow = ((2 * ROWS, DS), f32), ((ROWS, DS), bf16)
    block = ((ROWS, DS), f32)
    rows, col0 = pairs(own_kernel, [VMEM] * 3, [wide, block], [], OWN_COST, image_later, image_y, text_own)
    dp = lax.axis_index(DP) % 64
    place = pltpu.VMEM((ROWS + PAD, DT + DS), bf16)
    rows, col1, col2 = pairs(
        near_kernel,
        [SMEM] + [VMEM] * 7,
        [wide, block, narrow],
        [place] * 2,
        4,
        jnp.stack([dp == 0, dp == 1]).astype(jnp.int32),
        image_later,
        image_y,
        recv,
        aside,
        exch,
        aside_exch,
        rows,
    )
    both = (col1 + swap(col2, "core").astype(f32)).astype(bf16)
    both_back = chip_shift(both, -1)
    own_rows, other_rows, col3 = pairs(
        far_kernel,
        [SMEM] + [VMEM] * 5,
        [block, narrow, narrow],
        [place],
        FAR_COST,
        first.astype(jnp.int32)[None],
        image_later,
        image_y,
        beside,
        behind,
        rows,
    )
    far_back = along_dp(col3, back_route)
    rows_y = swap(other_rows, "yh")
    grad_img = own_rows + rows_y.astype(f32)
    grad_txt = col0 + both_back.astype(f32) + far_back.astype(f32)

    img_high, img_low = direction(image_unit, image_len, grad_img)
    txt_high, txt_low = direction(text_unit, text_len, grad_txt)
    high_in = swap(jnp.where(first, txt_high, img_high), "core")
    low_in = swap(jnp.where(first, txt_low, img_low), "core")
    high_own = jnp.where(first, img_high, txt_high)
    low_own = jnp.where(first, img_low, txt_low)
    feats2 = jnp.concatenate([kept_feats, feats_in], axis=0)
    high2 = jnp.concatenate([high_own, high_in], axis=0)
    low2 = jnp.concatenate([low_own, low_in], axis=0)
    dims = (((0,), (0,)), ((), ()))
    part = lax.dot_general(feats2, high2, dims, preferred_element_type=f32) + lax.dot_general(
        feats2, low2, dims, preferred_element_type=f32
    )
    own_total, other_total, own_e, other_e = sum_everywhere(part)
    own_total = own_total.astype(f32) * jnp.exp2(own_e)
    other_total = other_total.astype(f32) * jnp.exp2(other_e)
    return (
        jnp.where(first, own_total, other_total),
        jnp.where(first, other_total, own_total),
    )


def solution(mesh):
    fine = Mesh(mesh.devices.reshape(2, 8, 4, 2, 2), AXES)
    rows = P(AXES, None)
    in_specs = (rows, P(), rows, rows, rows, P(), P(), P(AXES))
    return jax.shard_map(
        local, mesh=fine, in_specs=in_specs, out_specs=(P(), P()), check_vma=False
    )
```

```python
import jax
import jax.numpy as jnp
from jax import lax
from jax.experimental import pallas as pl
from jax.experimental.pallas import tpu as pltpu
from jax.sharding import Mesh
from jax.sharding import PartitionSpec as P

epsilon = 1e-06
scale = 20.0
shift = -1.0

AXES = ("yl", "z", "x", "core", "yh")
DP = ("yl", "z", "x", "core")
N_DP = 128

f32 = jnp.float32
bf16 = jnp.bfloat16
f16 = jnp.float16


def unit_rows(raw_rows):
    row_len = jnp.sqrt(jnp.sum(raw_rows * raw_rows, axis=1, keepdims=True) + epsilon)
    return (raw_rows / row_len, row_len)


def swap(block, axis):
    return lax.ppermute(block, axis, [(0, 1), (1, 0)])


def along_dp(block, route):
    return lax.ppermute(block, DP, route)


def chip_shift(block, step):
    return along_dp(block, [(i, (i + 2 * step) % N_DP) for i in range(N_DP)])


EVEN_ON = [(i, i + 2) for i in range(0, N_DP, 2) if i not in (62, 126)] + [(126, 57), (62, 121)]
ODD_ON = [(i, (i + 2) % N_DP) for i in range(1, N_DP, 2)]
EVEN_OVER = [(i, i + 1) for i in range(0, N_DP, 2) if i not in (0, 64)] + [(57, 1), (121, 65)]
ODD_OVER = [(i, i - 1) for i in range(1, N_DP, 2)]
LAST_HOP = [(57, 0), (121, 64)]
EVEN_STEP = [(i, i + 1) for i in range(0, N_DP, 2)]
ODD_STEP = [(i, (i + 1) % N_DP) for i in range(1, N_DP, 2)]


VMEM = pl.BlockSpec(memory_space=pltpu.VMEM)
SMEM = pl.BlockSpec(memory_space=pltpu.SMEM)
ROWS = 256
DT = 1536
DS = 768
PAD = 16
VMEM_ALL = 61 * 2**20
FAR_COST = 40
OWN_COST = 2


def note_ids(ids, payload):
    payload[ROWS:, :] = jnp.zeros((PAD, DT + DS), bf16)
    payload[ROWS:, :ROWS] = jnp.broadcast_to(ids[...], (PAD, ROWS)).astype(f32).astype(bf16)


def student(feats, proj, payload, unit_out, len_out):
    unit, length = unit_rows(jnp.dot(feats[...], proj[...], preferred_element_type=f32))
    payload[:ROWS, DT:] = unit.astype(bf16)
    unit_out[...] = unit
    len_out[...] = length


def text_kernel(ids, feats, proj, teacher, payload, unit_out, len_out):
    student(feats, proj, payload, unit_out, len_out)
    unit, _ = unit_rows(teacher[...].astype(f32))
    payload[:ROWS, :DT] = unit.astype(bf16)
    note_ids(ids, payload)


def image_kernel(ids, feats, proj, teacher, teacher_proj, payload, unit_out, len_out):
    student(feats, proj, payload, unit_out, len_out)
    unit, _ = unit_rows(jnp.dot(teacher[...], teacher_proj[...], preferred_element_type=f32))
    payload[:ROWS, :DT] = unit.astype(bf16)
    note_ids(ids, payload)


def embed(kernel, flops, *args):
    return pl.pallas_call(
        kernel,
        in_specs=[VMEM] * len(args),
        out_specs=[VMEM] * 3,
        out_shape=[
            jax.ShapeDtypeStruct((ROWS + PAD, DT + DS), bf16),
            jax.ShapeDtypeStruct((ROWS, DS), f32),
            jax.ShapeDtypeStruct((ROWS, 1), f32),
        ],
        compiler_params=pltpu.CompilerParams(vmem_limit_bytes=VMEM_ALL),
        cost_estimate=pl.CostEstimate(flops=flops, bytes_accessed=5 * 2**20, transcendentals=0),
    )(*args)


CROSS = (((1,), (1,)), ((), ()))
OVER_ROWS = (((0,), (0,)), ((), ()))


def tile(image, text):
    teacher_dot = lax.dot_general(
        image[:ROWS, :DT], text[:ROWS, :DT], CROSS, preferred_element_type=f32
    )
    row_ids = jnp.broadcast_to(image[ROWS:, :ROWS].astype(f32)[:1], (ROWS, ROWS)).T
    labels = (row_ids == text[ROWS:, :ROWS].astype(f32)[:1]).astype(f32)
    target = 0.5 * jax.nn.sigmoid(scale * teacher_dot + shift) + 0.5 * labels
    logits = (
        scale
        * lax.dot_general(
            image[:ROWS, DT:], text[:ROWS, DT:], CROSS, preferred_element_type=f32
        )
        + shift
    )
    resid = ((jax.nn.sigmoid(logits) - target) * (1.0 / ROWS)).astype(bf16)
    row_part = scale * jnp.dot(resid, text[:ROWS, DT:], preferred_element_type=f32)
    col_part = scale * lax.dot_general(
        resid, image[:ROWS, DT:], OVER_ROWS, preferred_element_type=f32
    )
    return row_part, col_part


def own_kernel(own, other, text, rows, col):
    row_a, col_a = tile(own, text)
    rows[:ROWS] = row_a
    row_b, col_b = tile(other, text)
    rows[ROWS:] = row_b
    col[...] = col_a + col_b


def near_kernel(
    kind, own, other, even, odd, aside, even_over, odd_over, before, rows, col1, col2, recv, exch
):
    recv[...] = jnp.where(
        kind[0] == 2, odd[...], jnp.where(kind[0] == 1, aside[...], even[...])
    )
    exch[...] = jnp.where(kind[0] == 2, even_over[...], odd_over[...])
    row_a, col_a = tile(own, exch)
    row_b, col_b = tile(own, recv)
    rows[:ROWS] = row_a + row_b + before[:ROWS]
    row_a, col_c = tile(other, exch)
    row_b, col_d = tile(other, recv)
    rows[ROWS:] = row_a + row_b + before[ROWS:]
    col2[...] = (col_a + col_c).astype(bf16)
    col1[...] = col_b + col_d


def far_kernel(flag, own, other, beside, behind, rows, own_rows, other_rows, col, text):
    text[...] = jnp.where(flag[0] == 1, behind[...], beside[...])
    row_a, col_a = tile(own, text)
    row_b, col_b = tile(other, text)
    col[...] = (col_a + col_b).astype(bf16)
    own_rows[...] = row_a + rows[:ROWS]
    other_rows[...] = (row_b + rows[ROWS:]).astype(bf16)


def pairs(kernel, specs, outs, scratch, tiles, *args):
    return pl.pallas_call(
        kernel,
        in_specs=specs,
        out_specs=[VMEM] * len(outs),
        out_shape=[jax.ShapeDtypeStruct(shape, dtype) for shape, dtype in outs],
        scratch_shapes=scratch,
        compiler_params=pltpu.CompilerParams(vmem_limit_bytes=28 * 2**20),
        cost_estimate=pl.CostEstimate(
            flops=tiles * 10**9, bytes_accessed=tiles * 3 * 2**20, transcendentals=0
        ),
    )(*args)


def direction(unit, length, grad):
    d = (grad - unit * jnp.sum(unit * grad, axis=1, keepdims=True)) / length
    high = d.astype(bf16)
    low = (d - high.astype(f32)).astype(bf16)
    return high, low


def packed(values, exponent):
    scaled = (values * jnp.exp2(-exponent)).astype(f16)
    shape = (values.shape[0], 8, values.shape[2])
    note = jnp.broadcast_to(exponent.astype(f16), shape)
    return jnp.concatenate([scaled, note], axis=1)


def unpacked_sum(blocks):
    exponents = blocks[:, -8:-7, :].astype(f32)
    summed = (blocks[:, :-8].astype(f32) * jnp.exp2(exponents)).sum(axis=0)
    return summed, exponents.max(axis=0)


def sum_everywhere(part):
    ds = part.shape[0]
    biggest = jnp.log2(jnp.maximum(jnp.max(jnp.abs(part)), 1e-30))
    exponent = jnp.clip(jnp.ceil(biggest) - 14.0, -110.0, 110.0)
    blocks = packed(part.reshape(4, ds // 4, ds), exponent)
    blocks = lax.all_to_all(blocks, "x", 0, 0, tiled=True)
    summed, exponent = unpacked_sum(blocks)
    exponent = exponent + 2.0
    blocks = packed(summed.reshape(8, ds // 32, ds), exponent)
    blocks = lax.all_to_all(blocks, "z", 0, 0, tiled=True)
    summed, exponent = unpacked_sum(blocks)
    noted = jnp.concatenate([summed, jnp.broadcast_to(exponent, (8, ds))], axis=0)
    other_l = swap(noted, "yl")
    other_h = swap(noted, "yh")
    other_b = lax.ppermute(noted, ("yl", "yh"), [(0, 3), (1, 2), (2, 1), (3, 0)])
    summed = ((noted + other_l) + (other_h + other_b))[:-8]
    exponent = jnp.maximum(
        jnp.maximum(noted, other_l), jnp.maximum(other_h, other_b)
    )[-8:-7] + 5.0
    other_e = swap(jnp.broadcast_to(exponent, (8, ds)), "core")[0:1]
    block = (summed * jnp.exp2(-exponent)).astype(f16)
    spread = jnp.broadcast_to(block[None], (8,) + block.shape)
    gathered = lax.all_to_all(spread, "z", 0, 0, tiled=True).reshape(ds // 4, ds)
    spread = jnp.broadcast_to(gathered[None], (4,) + gathered.shape)
    own_total = lax.all_to_all(spread, "x", 0, 0, tiled=True).reshape(ds, ds)
    return own_total, swap(own_total, "core"), exponent, other_e


def local(
    teacher_image,
    teacher_proj,
    teacher_text,
    image_feats,
    text_feats,
    image_proj,
    text_proj,
    class_ids,
):
    core = lax.axis_index("core")
    first = core == 0
    back_route = [(i, i - 1 if i % 2 else (i - 3) % N_DP) for i in range(N_DP)]
    ids = class_ids[None, :]
    text_own, text_unit, text_len = embed(
        text_kernel, 10**9, ids, text_feats, text_proj, teacher_text
    )
    ids, image_feats, teacher_image, text_own = lax.optimization_barrier(
        (ids, image_feats, teacher_image, text_own)
    )
    even = along_dp(text_own, EVEN_ON)
    odd = along_dp(text_own, ODD_ON)
    beside = along_dp(text_own, EVEN_STEP)
    image_own, image_unit, image_len = embed(
        image_kernel, 2 * 10**9, ids, image_feats, image_proj, teacher_image, teacher_proj
    )
    image_y = swap(image_own, "yh")
    even, beside, image_later = lax.optimization_barrier((even, beside, image_own))
    even_over = along_dp(even, EVEN_OVER)
    aside = along_dp(even, LAST_HOP)
    odd, _ = lax.optimization_barrier((odd, image_own))
    behind = along_dp(odd, ODD_STEP)
    odd_over = along_dp(odd, ODD_OVER)

    sent_feats = jnp.where(first, text_feats, image_feats)
    kept_feats = jnp.where(first, image_feats, text_feats)
    feats_in = swap(sent_feats, "core")

    wide, narrow = ((2 * ROWS, DS), f32), ((ROWS, DS), bf16)
    block = ((ROWS, DS), f32)
    rows, col0 = pairs(own_kernel, [VMEM] * 3, [wide, block], [], OWN_COST, image_later, image_y, text_own)
    dp = lax.axis_index(DP) % 64
    place = pltpu.VMEM((ROWS + PAD, DT + DS), bf16)
    rows, col1, col2 = pairs(
        near_kernel,
        [SMEM] + [VMEM] * 8,
        [wide, block, narrow],
        [place] * 2,
        4,
        jnp.where(first, (dp == 0).astype(jnp.int32), 2)[None],
        image_later,
        image_y,
        even,
        odd,
        aside,
        even_over,
        odd_over,
        rows,
    )
    both = (col1 + swap(col2, "core").astype(f32)).astype(bf16)
    both_back = chip_shift(both, -1)
    own_rows, other_rows, col3 = pairs(
        far_kernel,
        [SMEM] + [VMEM] * 5,
        [block, narrow, narrow],
        [place],
        FAR_COST,
        first.astype(jnp.int32)[None],
        image_later,
        image_y,
        beside,
        behind,
        rows,
    )
    far_back = along_dp(col3, back_route)
    rows_y = swap(other_rows, "yh")
    grad_img = own_rows + rows_y.astype(f32)
    grad_txt = col0 + both_back.astype(f32) + far_back.astype(f32)

    img_high, img_low = direction(image_unit, image_len, grad_img)
    txt_high, txt_low = direction(text_unit, text_len, grad_txt)
    high_in = swap(jnp.where(first, txt_high, img_high), "core")
    low_in = swap(jnp.where(first, txt_low, img_low), "core")
    high_own = jnp.where(first, img_high, txt_high)
    low_own = jnp.where(first, img_low, txt_low)
    feats2 = jnp.concatenate([kept_feats, feats_in], axis=0)
    high2 = jnp.concatenate([high_own, high_in], axis=0)
    low2 = jnp.concatenate([low_own, low_in], axis=0)
    dims = (((0,), (0,)), ((), ()))
    part = lax.dot_general(feats2, high2, dims, preferred_element_type=f32) + lax.dot_general(
        feats2, low2, dims, preferred_element_type=f32
    )
    own_total, other_total, own_e, other_e = sum_everywhere(part)
    own_total = own_total.astype(f32) * jnp.exp2(own_e)
    other_total = other_total.astype(f32) * jnp.exp2(other_e)
    return (
        jnp.where(first, own_total, other_total),
        jnp.where(first, other_total, own_total),
    )


def solution(mesh):
    fine = Mesh(mesh.devices.reshape(2, 8, 4, 2, 2), AXES)
    rows = P(AXES, None)
    in_specs = (rows, P(), rows, rows, rows, P(), P(), P(AXES))
    return jax.shard_map(
        local, mesh=fine, in_specs=in_specs, out_specs=(P(), P()), check_vma=False
    )
```

```python
import jax
import jax.numpy as jnp
from jax import lax
from jax.experimental import pallas as pl
from jax.experimental.pallas import tpu as pltpu
from jax.sharding import Mesh
from jax.sharding import PartitionSpec as P

epsilon = 1e-06
scale = 20.0
shift = -1.0

AXES = ("yl", "z", "x", "core", "yh")
DP = ("yl", "z", "x", "core")
N_DP = 128
COST1 = 10**10
COST2 = 2 * 10**10

f32 = jnp.float32
bf16 = jnp.bfloat16
f16 = jnp.float16


def unit_rows(raw_rows):
    row_len = jnp.sqrt(jnp.sum(raw_rows * raw_rows, axis=1, keepdims=True) + epsilon)
    return (raw_rows / row_len, row_len)


def swap(block, axis):
    return lax.ppermute(block, axis, [(0, 1), (1, 0)])


def along_dp(block, route):
    return lax.ppermute(block, DP, route)


def chip_shift(block, step):
    return along_dp(block, [(i, (i + 2 * step) % N_DP) for i in range(N_DP)])


def hand_on_kernel(flag, own, got, onward):
    onward[...] = jnp.where(flag[0] == 1, own[...], got[...])


def hand_on(first, own, got, flops):
    block = pl.BlockSpec((own.shape[0] // 2, own.shape[1]), lambda i, flag: (i, 0))
    return pl.pallas_call(
        hand_on_kernel,
        grid_spec=pltpu.PrefetchScalarGridSpec(
            num_scalar_prefetch=1, grid=(2,), in_specs=[block] * 2, out_specs=block
        ),
        out_shape=jax.ShapeDtypeStruct(own.shape, own.dtype),
        cost_estimate=pl.CostEstimate(flops=flops, bytes_accessed=own.size * 6, transcendentals=0),
    )(first.astype(jnp.int32)[None], own, got)


def with_ids(rows, ids):
    below = jnp.pad(ids.astype(rows.dtype)[None, :], ((0, 15), (0, rows.shape[1] - ids.shape[0])))
    return jnp.concatenate([rows, below], axis=0)


def without_ids(noted):
    count = noted.shape[0] - 16
    return noted[:count], noted[count, :count]


def pair_tile(teach_rows, image_rows, row_ids, teach_cols, noted_cols):
    text_cols, col_ids = without_ids(noted_cols)
    wide = teach_cols.astype(f32)
    inverse = 1.0 / jnp.sqrt(jnp.sum(wide * wide, axis=1) + epsilon)
    teacher_dot = (
        lax.dot_general(
            teach_rows, teach_cols, (((1,), (1,)), ((), ())), preferred_element_type=f32
        )
        * inverse[None, :]
    )
    labels = (row_ids == col_ids[None, :]).astype(f32)
    target = 0.5 * jax.nn.sigmoid(scale * teacher_dot + shift) + 0.5 * labels
    logits = (
        scale
        * lax.dot_general(
            image_rows, text_cols, (((1,), (1,)), ((), ())), preferred_element_type=f32
        )
        + shift
    )
    scaled = ((jax.nn.sigmoid(logits) - target) / text_cols.shape[0]).astype(bf16)
    row_part = scale * jnp.dot(scaled, text_cols, preferred_element_type=f32)
    col_part = scale * lax.dot_general(
        scaled, image_rows, (((0,), (0,)), ((), ())), preferred_element_type=f32
    )
    return (row_part, col_part)


def direction(unit, length, grad):
    d = (grad - unit * jnp.sum(unit * grad, axis=1, keepdims=True)) / length
    high = d.astype(bf16)
    low = (d - high.astype(f32)).astype(bf16)
    return high, low


def packed(values, exponent):
    scaled = (values * jnp.exp2(-exponent)).astype(f16)
    shape = (values.shape[0], 8, values.shape[2])
    note = jnp.broadcast_to(exponent.astype(f16), shape)
    return jnp.concatenate([scaled, note], axis=1)


def unpacked_sum(blocks):
    exponents = blocks[:, -8:-7, :].astype(f32)
    summed = (blocks[:, :-8].astype(f32) * jnp.exp2(exponents)).sum(axis=0)
    return summed, exponents.max(axis=0)


def sum_everywhere(part):
    ds = part.shape[0]
    biggest = jnp.log2(jnp.maximum(jnp.max(jnp.abs(part)), 1e-30))
    exponent = jnp.clip(jnp.ceil(biggest) - 14.0, -110.0, 110.0)
    blocks = packed(part.reshape(4, ds // 4, ds), exponent)
    blocks = lax.all_to_all(blocks, "x", 0, 0, tiled=True)
    summed, exponent = unpacked_sum(blocks)
    exponent = exponent + 2.0
    blocks = packed(summed.reshape(8, ds // 32, ds), exponent)
    blocks = lax.all_to_all(blocks, "z", 0, 0, tiled=True)
    summed, exponent = unpacked_sum(blocks)
    noted = jnp.concatenate([summed, jnp.broadcast_to(exponent, (8, ds))], axis=0)
    other_l = swap(noted, "yl")
    other_h = swap(noted, "yh")
    other_b = lax.ppermute(noted, ("yl", "yh"), [(0, 3), (1, 2), (2, 1), (3, 0)])
    summed = ((noted + other_l) + (other_h + other_b))[:-8]
    exponent = jnp.maximum(
        jnp.maximum(noted, other_l), jnp.maximum(other_h, other_b)
    )[-8:-7] + 5.0
    other_e = swap(jnp.broadcast_to(exponent, (8, ds)), "core")[0:1]
    block = (summed * jnp.exp2(-exponent)).astype(f16)
    spread = jnp.broadcast_to(block[None], (8,) + block.shape)
    gathered = lax.all_to_all(spread, "z", 0, 0, tiled=True).reshape(ds // 4, ds)
    spread = jnp.broadcast_to(gathered[None], (4,) + gathered.shape)
    own_total = lax.all_to_all(spread, "x", 0, 0, tiled=True).reshape(ds, ds)
    return own_total, swap(own_total, "core"), exponent, other_e


def local(
    teacher_image,
    teacher_proj,
    teacher_text,
    image_feats,
    text_feats,
    image_proj,
    text_proj,
    class_ids,
):
    core = lax.axis_index("core")
    first = core == 0
    back_route = [(i, i - 1 if i % 2 else (i - 3) % N_DP) for i in range(N_DP)]
    step_route = [(i, (i + 1) % N_DP) for i in range(N_DP)]

    teach_recv = chip_shift(teacher_text, 1)
    teach_y = swap(teacher_image, "yh")
    text_unit, text_len = unit_rows(jnp.dot(text_feats, text_proj, preferred_element_type=f32))
    text_own = with_ids(text_unit.astype(bf16), class_ids)
    image_first, text_own = lax.optimization_barrier((image_feats, text_own))
    text_recv = chip_shift(text_own, 1)
    image_unit, image_len = unit_rows(
        jnp.dot(image_first, image_proj, preferred_element_type=f32)
    )
    image_own = with_ids(image_unit.astype(bf16), class_ids)
    teacher_later, image_own = lax.optimization_barrier((teacher_image, image_own))
    image_y = swap(image_own, "yh")
    teach_on = hand_on(first, teacher_text, teach_recv, COST2)
    text_on = hand_on(first, text_own, text_recv, COST1)
    teach_far = along_dp(teach_on, step_route)
    text_far = along_dp(text_on, step_route)
    teach_y, image_y, _, _ = lax.optimization_barrier((teach_y, image_y, teach_on, text_on))
    text_exch = swap(text_recv, "core")
    teach_exch = swap(teach_recv, "core")

    def teacher_rows(rows):
        unit, _ = unit_rows(jnp.dot(rows, teacher_proj, preferred_element_type=f32))
        return unit.astype(bf16)

    teacher_img = teacher_rows(teacher_later)
    teacher_img_y = teacher_rows(teach_y)

    sent_feats = jnp.where(first, text_feats, image_feats)
    kept_feats = jnp.where(first, image_feats, text_feats)
    feats_in = swap(sent_feats, "core")

    image_emb, ids = without_ids(image_own)
    image_emb_y, ids_y = without_ids(image_y)
    image_rows = jnp.concatenate([image_emb, image_emb_y], axis=0)
    teach_rows = jnp.concatenate([teacher_img, teacher_img_y], axis=0)
    row_ids = jnp.concatenate([ids, ids_y], axis=0)[:, None]
    rows = (teach_rows, image_rows, row_ids)
    row0, col0 = pair_tile(*rows, teacher_text, text_own)
    row1, col1 = pair_tile(*rows, teach_recv, text_recv)
    row2, col2 = pair_tile(*rows, teach_exch, text_exch)
    both = col1 + swap(col2.astype(bf16), "core").astype(f32)
    both_back = chip_shift(both.astype(bf16), -1)
    row3, col3 = pair_tile(*rows, teach_far, text_far)
    far_back = along_dp(col3.astype(bf16), back_route)
    grad_rows = row0 + row1 + row2 + row3
    half = image_emb.shape[0]
    rows_y = swap(grad_rows[half:].astype(bf16), "yh")
    grad_img = grad_rows[:half] + rows_y.astype(f32)
    grad_txt = col0 + both_back.astype(f32) + far_back.astype(f32)

    img_high, img_low = direction(image_unit, image_len, grad_img)
    txt_high, txt_low = direction(text_unit, text_len, grad_txt)
    high_in = swap(jnp.where(first, txt_high, img_high), "core")
    low_in = swap(jnp.where(first, txt_low, img_low), "core")
    high_own = jnp.where(first, img_high, txt_high)
    low_own = jnp.where(first, img_low, txt_low)
    feats2 = jnp.concatenate([kept_feats, feats_in], axis=0)
    high2 = jnp.concatenate([high_own, high_in], axis=0)
    low2 = jnp.concatenate([low_own, low_in], axis=0)
    dims = (((0,), (0,)), ((), ()))
    part = lax.dot_general(feats2, high2, dims, preferred_element_type=f32) + lax.dot_general(
        feats2, low2, dims, preferred_element_type=f32
    )
    own_total, other_total, own_e, other_e = sum_everywhere(part)
    own_total = own_total.astype(f32) * jnp.exp2(own_e)
    other_total = other_total.astype(f32) * jnp.exp2(other_e)
    return (
        jnp.where(first, own_total, other_total),
        jnp.where(first, other_total, own_total),
    )


def solution(mesh):
    fine = Mesh(mesh.devices.reshape(2, 8, 4, 2, 2), AXES)
    rows = P(AXES, None)
    in_specs = (rows, P(), rows, rows, rows, P(), P(), P(AXES))
    return jax.shard_map(
        local, mesh=fine, in_specs=in_specs, out_specs=(P(), P()), check_vma=False
    )
```

```python
import jax
import jax.numpy as jnp
from jax import lax
from jax.sharding import Mesh
from jax.sharding import PartitionSpec as P

epsilon = 1e-06
scale = 20.0
shift = -1.0

AXES = ("yl", "z", "x", "core", "yh")
DP = ("yl", "z", "x", "core")
N_DP = 128

f32 = jnp.float32
bf16 = jnp.bfloat16
f16 = jnp.float16


def unit_rows(raw_rows):
    row_len = jnp.sqrt(jnp.sum(raw_rows * raw_rows, axis=1, keepdims=True) + epsilon)
    return (raw_rows / row_len, row_len)


def swap(block, axis):
    return lax.ppermute(block, axis, [(0, 1), (1, 0)])


def along_dp(block, route):
    return lax.ppermute(block, DP, route)


def chip_shift(block, step):
    return along_dp(block, [(i, (i + 2 * step) % N_DP) for i in range(N_DP)])


def pair_tile(target_rows, image_rows, row_ids, target_cols, text_cols, col_ids):
    teacher_dot = lax.dot_general(
        target_rows, target_cols, (((1,), (1,)), ((), ())), preferred_element_type=f32
    )
    labels = (row_ids[:, None] == col_ids[None, :]).astype(f32)
    target = 0.5 * jax.nn.sigmoid(scale * teacher_dot + shift) + 0.5 * labels
    logits = (
        scale
        * lax.dot_general(
            image_rows, text_cols, (((1,), (1,)), ((), ())), preferred_element_type=f32
        )
        + shift
    )
    scaled = ((jax.nn.sigmoid(logits) - target) / text_cols.shape[0]).astype(bf16)
    row_part = scale * jnp.dot(scaled, text_cols, preferred_element_type=f32)
    col_part = scale * lax.dot_general(
        scaled, image_rows, (((0,), (0,)), ((), ())), preferred_element_type=f32
    )
    return (row_part, col_part)


def direction(unit, length, grad):
    d = (grad - unit * jnp.sum(unit * grad, axis=1, keepdims=True)) / length
    high = d.astype(bf16)
    low = (d - high.astype(f32)).astype(bf16)
    return high, low


def packed(values, exponent):
    scaled = (values * jnp.exp2(-exponent)).astype(f16)
    shape = (values.shape[0], 8, values.shape[2])
    note = jnp.broadcast_to(exponent.astype(f16), shape)
    return jnp.concatenate([scaled, note], axis=1)


def unpacked_sum(blocks):
    exponents = blocks[:, -8:-7, :].astype(f32)
    summed = (blocks[:, :-8].astype(f32) * jnp.exp2(exponents)).sum(axis=0)
    return summed, exponents.max(axis=0)


def sum_everywhere(part):
    ds = part.shape[0]
    biggest = jnp.log2(jnp.maximum(jnp.max(jnp.abs(part)), 1e-30))
    exponent = jnp.clip(jnp.ceil(biggest) - 14.0, -110.0, 110.0)
    blocks = packed(part.reshape(4, ds // 4, ds), exponent)
    blocks = lax.all_to_all(blocks, "x", 0, 0, tiled=True)
    summed, exponent = unpacked_sum(blocks)
    exponent = exponent + 2.0
    blocks = packed(summed.reshape(8, ds // 32, ds), exponent)
    blocks = lax.all_to_all(blocks, "z", 0, 0, tiled=True)
    summed, exponent = unpacked_sum(blocks)
    noted = jnp.concatenate([summed, jnp.broadcast_to(exponent, (8, ds))], axis=0)
    other_l = swap(noted, "yl")
    other_h = swap(noted, "yh")
    other_b = lax.ppermute(noted, ("yl", "yh"), [(0, 3), (1, 2), (2, 1), (3, 0)])
    summed = ((noted + other_l) + (other_h + other_b))[:-8]
    exponent = jnp.maximum(
        jnp.maximum(noted, other_l), jnp.maximum(other_h, other_b)
    )[-8:-7] + 5.0
    other_e = swap(jnp.broadcast_to(exponent, (8, ds)), "core")[0:1]
    block = (summed * jnp.exp2(-exponent)).astype(f16)
    spread = jnp.broadcast_to(block[None], (8,) + block.shape)
    gathered = lax.all_to_all(spread, "z", 0, 0, tiled=True).reshape(ds // 4, ds)
    spread = jnp.broadcast_to(gathered[None], (4,) + gathered.shape)
    own_total = lax.all_to_all(spread, "x", 0, 0, tiled=True).reshape(ds, ds)
    return own_total, swap(own_total, "core"), exponent, other_e


def local(
    teacher_image,
    teacher_proj,
    teacher_text,
    image_feats,
    text_feats,
    image_proj,
    text_proj,
    class_ids,
):
    core = lax.axis_index("core")
    first = core == 0
    back_route = [(i, i - 1 if i % 2 else (i - 3) % N_DP) for i in range(N_DP)]
    step_route = [(i, (i + 1) % N_DP) for i in range(N_DP)]

    ids_y = swap(class_ids, "yh")
    ids1 = along_dp(class_ids, step_route)
    ids2 = along_dp(class_ids, [(i, (i + 2) % N_DP) for i in range(N_DP)])
    ids3 = along_dp(class_ids, [(i, (i + 3) % N_DP) for i in range(N_DP)])

    text_unit, text_len = unit_rows(jnp.dot(text_feats, text_proj, preferred_element_type=f32))
    text_emb = text_unit.astype(bf16)
    text_recv = chip_shift(text_emb, 1)
    image_unit, image_len = unit_rows(
        jnp.dot(image_feats, image_proj, preferred_element_type=f32)
    )
    image_emb = image_unit.astype(bf16)
    image_y = swap(image_emb, "yh")
    written_unit, _ = unit_rows(teacher_text.astype(f32))
    teacher_txt = written_unit.astype(bf16)
    teach_recv = chip_shift(teacher_txt, 1)
    teacher_unit, _ = unit_rows(jnp.dot(teacher_image, teacher_proj, preferred_element_type=f32))
    teacher_img = teacher_unit.astype(bf16)
    teach_y = swap(teacher_img, "yh")
    text_exch = swap(text_recv, "core")
    text_far = along_dp(jnp.where(first, text_emb, text_recv), step_route)
    teach_exch = swap(teach_recv, "core")
    teach_far = along_dp(jnp.where(first, teacher_txt, teach_recv), step_route)

    sent_feats = jnp.where(first, text_feats, image_feats)
    kept_feats = jnp.where(first, image_feats, text_feats)
    feats_in = swap(sent_feats, "core")

    image_rows = jnp.concatenate([image_emb, image_y], axis=0)
    teach_rows = jnp.concatenate([teacher_img, teach_y], axis=0)
    row_ids = jnp.concatenate([class_ids, ids_y], axis=0)
    row0, col0 = pair_tile(teach_rows, image_rows, row_ids, teacher_txt, text_emb, class_ids)
    row1, col1 = pair_tile(teach_rows, image_rows, row_ids, teach_recv, text_recv, ids2)
    ids_exch = jnp.where(first, ids1, ids3)
    row2, col2 = pair_tile(teach_rows, image_rows, row_ids, teach_exch, text_exch, ids_exch)
    both = col1 + swap(col2.astype(bf16), "core").astype(f32)
    both_back = chip_shift(both.astype(bf16), -1)
    ids_far = jnp.where(first, ids3, ids1)
    row3, col3 = pair_tile(teach_rows, image_rows, row_ids, teach_far, text_far, ids_far)
    far_back = along_dp(col3.astype(bf16), back_route)
    grad_rows = row0 + row1 + row2 + row3
    half = text_emb.shape[0]
    rows_y = swap(grad_rows[half:].astype(bf16), "yh")
    grad_img = grad_rows[:half] + rows_y.astype(f32)
    grad_txt = col0 + both_back.astype(f32) + far_back.astype(f32)

    img_high, img_low = direction(image_unit, image_len, grad_img)
    txt_high, txt_low = direction(text_unit, text_len, grad_txt)
    high_in = swap(jnp.where(first, txt_high, img_high), "core")
    low_in = swap(jnp.where(first, txt_low, img_low), "core")
    high_own = jnp.where(first, img_high, txt_high)
    low_own = jnp.where(first, img_low, txt_low)
    feats2 = jnp.concatenate([kept_feats, feats_in], axis=0)
    high2 = jnp.concatenate([high_own, high_in], axis=0)
    low2 = jnp.concatenate([low_own, low_in], axis=0)
    dims = (((0,), (0,)), ((), ()))
    part = lax.dot_general(feats2, high2, dims, preferred_element_type=f32) + lax.dot_general(
        feats2, low2, dims, preferred_element_type=f32
    )
    own_total, other_total, own_e, other_e = sum_everywhere(part)
    own_total = own_total.astype(f32) * jnp.exp2(own_e)
    other_total = other_total.astype(f32) * jnp.exp2(other_e)
    return (
        jnp.where(first, own_total, other_total),
        jnp.where(first, other_total, own_total),
    )


def solution(mesh):
    fine = Mesh(mesh.devices.reshape(2, 8, 4, 2, 2), AXES)
    rows = P(AXES, None)
    in_specs = (rows, P(), rows, rows, rows, P(), P(), P(AXES))
    return jax.shard_map(
        local, mesh=fine, in_specs=in_specs, out_specs=(P(), P()), check_vma=False
    )
```

```python
import jax
import jax.numpy as jnp
from jax import lax
from jax.sharding import Mesh
from jax.sharding import PartitionSpec as P

epsilon = 1e-06
scale = 20.0
shift = -1.0

AXES = ("yl", "z", "x", "core", "yh")
DP = ("yl", "z", "x", "core")
N_DP = 128

f32 = jnp.float32
bf16 = jnp.bfloat16
f16 = jnp.float16


def unit_rows(raw_rows):
    row_len = jnp.sqrt(jnp.sum(raw_rows * raw_rows, axis=1, keepdims=True) + epsilon)
    return (raw_rows / row_len, row_len)


def swap(block, axis):
    return lax.ppermute(block, axis, [(0, 1), (1, 0)])


def along_dp(block, route):
    return lax.ppermute(block, DP, route)


def chip_shift(block, step):
    return along_dp(block, [(i, (i + 2 * step) % N_DP) for i in range(N_DP)])


def pair_tile(target_rows, image_rows, row_ids, target_cols, text_cols, col_ids):
    wide = target_cols.astype(f32)
    inverse = 1.0 / jnp.sqrt(jnp.sum(wide * wide, axis=1) + epsilon)
    teacher_dot = inverse[None, :] * lax.dot_general(
        target_rows, target_cols, (((1,), (1,)), ((), ())), preferred_element_type=f32
    )
    labels = (row_ids[:, None] == col_ids[None, :]).astype(f32)
    target = 0.5 * jax.nn.sigmoid(scale * teacher_dot + shift) + 0.5 * labels
    logits = (
        scale
        * lax.dot_general(
            image_rows, text_cols, (((1,), (1,)), ((), ())), preferred_element_type=f32
        )
        + shift
    )
    scaled = ((jax.nn.sigmoid(logits) - target) / text_cols.shape[0]).astype(bf16)
    row_part = scale * jnp.dot(scaled, text_cols, preferred_element_type=f32)
    col_part = scale * lax.dot_general(
        scaled, image_rows, (((0,), (0,)), ((), ())), preferred_element_type=f32
    )
    return (row_part, col_part)


def direction(unit, length, grad):
    d = (grad - unit * jnp.sum(unit * grad, axis=1, keepdims=True)) / length
    high = d.astype(bf16)
    low = (d - high.astype(f32)).astype(bf16)
    return high, low


def packed(values, exponent):
    scaled = (values * jnp.exp2(-exponent)).astype(f16)
    shape = (values.shape[0], 8, values.shape[2])
    note = jnp.broadcast_to(exponent.astype(f16), shape)
    return jnp.concatenate([scaled, note], axis=1)


def unpacked_sum(blocks):
    exponents = blocks[:, -8:-7, :].astype(f32)
    summed = (blocks[:, :-8].astype(f32) * jnp.exp2(exponents)).sum(axis=0)
    return summed, exponents.max(axis=0)


def sum_everywhere(part):
    ds = part.shape[0]
    biggest = jnp.log2(jnp.maximum(jnp.max(jnp.abs(part)), 1e-30))
    exponent = jnp.clip(jnp.ceil(biggest) - 14.0, -110.0, 110.0)
    blocks = packed(part.reshape(4, ds // 4, ds), exponent)
    blocks = lax.all_to_all(blocks, "x", 0, 0, tiled=True)
    summed, exponent = unpacked_sum(blocks)
    exponent = exponent + 2.0
    blocks = packed(summed.reshape(8, ds // 32, ds), exponent)
    blocks = lax.all_to_all(blocks, "z", 0, 0, tiled=True)
    summed, exponent = unpacked_sum(blocks)
    noted = jnp.concatenate([summed, jnp.broadcast_to(exponent, (8, ds))], axis=0)
    other_l = swap(noted, "yl")
    other_h = swap(noted, "yh")
    other_b = lax.ppermute(noted, ("yl", "yh"), [(0, 3), (1, 2), (2, 1), (3, 0)])
    summed = ((noted + other_l) + (other_h + other_b))[:-8]
    exponent = jnp.maximum(
        jnp.maximum(noted, other_l), jnp.maximum(other_h, other_b)
    )[-8:-7] + 5.0
    other_e = swap(jnp.broadcast_to(exponent, (8, ds)), "core")[0:1]
    block = (summed * jnp.exp2(-exponent)).astype(f16)
    spread = jnp.broadcast_to(block[None], (8,) + block.shape)
    gathered = lax.all_to_all(spread, "z", 0, 0, tiled=True).reshape(ds // 4, ds)
    spread = jnp.broadcast_to(gathered[None], (4,) + gathered.shape)
    own_total = lax.all_to_all(spread, "x", 0, 0, tiled=True).reshape(ds, ds)
    return own_total, swap(own_total, "core"), exponent, other_e


def local(
    teacher_image,
    teacher_proj,
    teacher_text,
    image_feats,
    text_feats,
    image_proj,
    text_proj,
    class_ids,
):
    core = lax.axis_index("core")
    first = core == 0
    back_route = [(i, i - 1 if i % 2 else (i - 3) % N_DP) for i in range(N_DP)]
    step_route = [(i, (i + 1) % N_DP) for i in range(N_DP)]

    ids_y = swap(class_ids, "yh")
    ids1 = along_dp(class_ids, step_route)
    ids2 = along_dp(class_ids, [(i, (i + 2) % N_DP) for i in range(N_DP)])
    ids3 = along_dp(class_ids, [(i, (i + 3) % N_DP) for i in range(N_DP)])

    text_unit, text_len = unit_rows(jnp.dot(text_feats, text_proj, preferred_element_type=f32))
    text_emb = text_unit.astype(bf16)
    text_recv = chip_shift(text_emb, 1)
    image_unit, image_len = unit_rows(
        jnp.dot(image_feats, image_proj, preferred_element_type=f32)
    )
    image_emb = image_unit.astype(bf16)
    image_y = swap(image_emb, "yh")
    teach_recv = chip_shift(teacher_text, 1)
    teacher_unit, _ = unit_rows(jnp.dot(teacher_image, teacher_proj, preferred_element_type=f32))
    teacher_img = teacher_unit.astype(bf16)
    teach_y = swap(teacher_img, "yh")
    text_exch = swap(text_recv, "core")
    text_far = along_dp(jnp.where(first, text_emb, text_recv), step_route)
    teach_exch = swap(teach_recv, "core")
    teach_far = along_dp(jnp.where(first, teacher_text, teach_recv), step_route)

    sent_feats = jnp.where(first, text_feats, image_feats)
    kept_feats = jnp.where(first, image_feats, text_feats)
    feats_in = swap(sent_feats, "core")

    image_rows = jnp.concatenate([image_emb, image_y], axis=0)
    teach_rows = jnp.concatenate([teacher_img, teach_y], axis=0)
    row_ids = jnp.concatenate([class_ids, ids_y], axis=0)
    row0, col0 = pair_tile(teach_rows, image_rows, row_ids, teacher_text, text_emb, class_ids)
    row1, col1 = pair_tile(teach_rows, image_rows, row_ids, teach_recv, text_recv, ids2)
    ids_exch = jnp.where(first, ids1, ids3)
    row2, col2 = pair_tile(teach_rows, image_rows, row_ids, teach_exch, text_exch, ids_exch)
    both = col1 + swap(col2.astype(bf16), "core").astype(f32)
    both_back = chip_shift(both.astype(bf16), -1)
    ids_far = jnp.where(first, ids3, ids1)
    row3, col3 = pair_tile(teach_rows, image_rows, row_ids, teach_far, text_far, ids_far)
    far_back = along_dp(col3.astype(bf16), back_route)
    grad_rows = row0 + row1 + row2 + row3
    half = text_emb.shape[0]
    rows_y = swap(grad_rows[half:].astype(bf16), "yh")
    grad_img = grad_rows[:half] + rows_y.astype(f32)
    grad_txt = col0 + both_back.astype(f32) + far_back.astype(f32)

    img_high, img_low = direction(image_unit, image_len, grad_img)
    txt_high, txt_low = direction(text_unit, text_len, grad_txt)
    high_in = swap(jnp.where(first, txt_high, img_high), "core")
    low_in = swap(jnp.where(first, txt_low, img_low), "core")
    high_own = jnp.where(first, img_high, txt_high)
    low_own = jnp.where(first, img_low, txt_low)
    feats2 = jnp.concatenate([kept_feats, feats_in], axis=0)
    high2 = jnp.concatenate([high_own, high_in], axis=0)
    low2 = jnp.concatenate([low_own, low_in], axis=0)
    dims = (((0,), (0,)), ((), ()))
    part = lax.dot_general(feats2, high2, dims, preferred_element_type=f32) + lax.dot_general(
        feats2, low2, dims, preferred_element_type=f32
    )
    own_total, other_total, own_e, other_e = sum_everywhere(part)
    own_total = own_total.astype(f32) * jnp.exp2(own_e)
    other_total = other_total.astype(f32) * jnp.exp2(other_e)
    return (
        jnp.where(first, own_total, other_total),
        jnp.where(first, other_total, own_total),
    )


def solution(mesh):
    fine = Mesh(mesh.devices.reshape(2, 8, 4, 2, 2), AXES)
    rows = P(AXES, None)
    in_specs = (rows, P(), rows, rows, rows, P(), P(), P(AXES))
    return jax.shard_map(
        local, mesh=fine, in_specs=in_specs, out_specs=(P(), P()), check_vma=False
    )
```

```python
import jax
import jax.numpy as jnp
from jax import lax
from jax.sharding import Mesh
from jax.sharding import PartitionSpec as P

epsilon = 1e-06
scale = 20.0
shift = -1.0

AXES = ("yl", "z", "x", "core", "yh")
DP = ("yl", "z", "x", "core")
N_DP = 128

f32 = jnp.float32
bf16 = jnp.bfloat16
f16 = jnp.float16


def unit_rows(raw_rows):
    row_len = jnp.sqrt(jnp.sum(raw_rows * raw_rows, axis=1, keepdims=True) + epsilon)
    return (raw_rows / row_len, row_len)


def swap(block, axis):
    return lax.ppermute(block, axis, [(0, 1), (1, 0)])


def along_dp(block, route):
    return lax.ppermute(block, DP, route)


def chip_shift(block, step):
    return along_dp(block, [(i, (i + 2 * step) % N_DP) for i in range(N_DP)])


def with_ids(rows, ids):
    below = jnp.pad(ids.astype(rows.dtype)[None, :], ((0, 15), (0, rows.shape[1] - ids.shape[0])))
    return jnp.concatenate([rows, below], axis=0)


def without_ids(noted):
    count = noted.shape[0] - 16
    return noted[:count], noted[count, :count]


def pair_tile(target_rows, image_rows, row_ids, target_cols, noted_cols):
    text_cols, col_ids = without_ids(noted_cols)
    wide = target_cols.astype(f32)
    inverse = 1.0 / jnp.sqrt(jnp.sum(wide * wide, axis=1) + epsilon)
    teacher_dot = inverse[None, :] * lax.dot_general(
        target_rows, target_cols, (((1,), (1,)), ((), ())), preferred_element_type=f32
    )
    labels = (row_ids[:, None] == col_ids[None, :]).astype(f32)
    target = 0.5 * jax.nn.sigmoid(scale * teacher_dot + shift) + 0.5 * labels
    logits = (
        scale
        * lax.dot_general(
            image_rows, text_cols, (((1,), (1,)), ((), ())), preferred_element_type=f32
        )
        + shift
    )
    scaled = ((jax.nn.sigmoid(logits) - target) / text_cols.shape[0]).astype(bf16)
    row_part = scale * jnp.dot(scaled, text_cols, preferred_element_type=f32)
    col_part = scale * lax.dot_general(
        scaled, image_rows, (((0,), (0,)), ((), ())), preferred_element_type=f32
    )
    return (row_part, col_part)


def direction(unit, length, grad):
    d = (grad - unit * jnp.sum(unit * grad, axis=1, keepdims=True)) / length
    high = d.astype(bf16)
    low = (d - high.astype(f32)).astype(bf16)
    return high, low


def packed(values, exponent):
    scaled = (values * jnp.exp2(-exponent)).astype(f16)
    shape = (values.shape[0], 8, values.shape[2])
    note = jnp.broadcast_to(exponent.astype(f16), shape)
    return jnp.concatenate([scaled, note], axis=1)


def unpacked_sum(blocks):
    exponents = blocks[:, -8:-7, :].astype(f32)
    summed = (blocks[:, :-8].astype(f32) * jnp.exp2(exponents)).sum(axis=0)
    return summed, exponents.max(axis=0)


def sum_everywhere(part):
    ds = part.shape[0]
    biggest = jnp.log2(jnp.maximum(jnp.max(jnp.abs(part)), 1e-30))
    exponent = jnp.clip(jnp.ceil(biggest) - 14.0, -110.0, 110.0)
    blocks = packed(part.reshape(4, ds // 4, ds), exponent)
    blocks = lax.all_to_all(blocks, "x", 0, 0, tiled=True)
    summed, exponent = unpacked_sum(blocks)
    exponent = exponent + 2.0
    blocks = packed(summed.reshape(8, ds // 32, ds), exponent)
    blocks = lax.all_to_all(blocks, "z", 0, 0, tiled=True)
    summed, exponent = unpacked_sum(blocks)
    noted = jnp.concatenate([summed, jnp.broadcast_to(exponent, (8, ds))], axis=0)
    other_l = swap(noted, "yl")
    other_h = swap(noted, "yh")
    other_b = lax.ppermute(noted, ("yl", "yh"), [(0, 3), (1, 2), (2, 1), (3, 0)])
    summed = ((noted + other_l) + (other_h + other_b))[:-8]
    exponent = jnp.maximum(
        jnp.maximum(noted, other_l), jnp.maximum(other_h, other_b)
    )[-8:-7] + 5.0
    other_e = swap(jnp.broadcast_to(exponent, (8, ds)), "core")[0:1]
    block = (summed * jnp.exp2(-exponent)).astype(f16)
    spread = jnp.broadcast_to(block[None], (8,) + block.shape)
    gathered = lax.all_to_all(spread, "z", 0, 0, tiled=True).reshape(ds // 4, ds)
    spread = jnp.broadcast_to(gathered[None], (4,) + gathered.shape)
    own_total = lax.all_to_all(spread, "x", 0, 0, tiled=True).reshape(ds, ds)
    return own_total, swap(own_total, "core"), exponent, other_e


def local(
    teacher_image,
    teacher_proj,
    teacher_text,
    image_feats,
    text_feats,
    image_proj,
    text_proj,
    class_ids,
):
    core = lax.axis_index("core")
    first = core == 0
    back_route = [(i, i - 1 if i % 2 else (i - 3) % N_DP) for i in range(N_DP)]
    step_route = [(i, (i + 1) % N_DP) for i in range(N_DP)]

    text_unit, text_len = unit_rows(jnp.dot(text_feats, text_proj, preferred_element_type=f32))
    text_own = with_ids(text_unit.astype(bf16), class_ids)
    text_recv = chip_shift(text_own, 1)
    teacher_later, text_own = lax.optimization_barrier((teacher_image, text_own))
    teacher_unit, _ = unit_rows(jnp.dot(teacher_later, teacher_proj, preferred_element_type=f32))
    teacher_img = teacher_unit.astype(bf16)
    image_later, teacher_img = lax.optimization_barrier((image_feats, teacher_img))
    teach_y = swap(teacher_img, "yh")
    image_unit, image_len = unit_rows(
        jnp.dot(image_later, image_proj, preferred_element_type=f32)
    )
    image_own = with_ids(image_unit.astype(bf16), class_ids)
    image_own, _ = lax.optimization_barrier((image_own, text_own))
    image_y = swap(image_own, "yh")
    teach_recv = chip_shift(teacher_text, 1)
    text_exch = swap(text_recv, "core")
    text_far = along_dp(jnp.where(first, text_own, text_recv), step_route)
    teach_exch = swap(teach_recv, "core")
    teach_far = along_dp(jnp.where(first, teacher_text, teach_recv), step_route)

    sent_feats = jnp.where(first, text_feats, image_feats)
    kept_feats = jnp.where(first, image_feats, text_feats)
    feats_in = swap(sent_feats, "core")

    image_emb, ids = without_ids(image_own)
    image_emb_y, ids_y = without_ids(image_y)
    image_rows = jnp.concatenate([image_emb, image_emb_y], axis=0)
    teach_rows = jnp.concatenate([teacher_img, teach_y], axis=0)
    row_ids = jnp.concatenate([ids, ids_y], axis=0)
    row0, col0 = pair_tile(teach_rows, image_rows, row_ids, teacher_text, text_own)
    row1, col1 = pair_tile(teach_rows, image_rows, row_ids, teach_recv, text_recv)
    row2, col2 = pair_tile(teach_rows, image_rows, row_ids, teach_exch, text_exch)
    both = col1 + swap(col2.astype(bf16), "core").astype(f32)
    both_back = chip_shift(both.astype(bf16), -1)
    row3, col3 = pair_tile(teach_rows, image_rows, row_ids, teach_far, text_far)
    far_back = along_dp(col3.astype(bf16), back_route)
    grad_rows = row0 + row1 + row2 + row3
    half = image_emb.shape[0]
    rows_y = swap(grad_rows[half:].astype(bf16), "yh")
    grad_img = grad_rows[:half] + rows_y.astype(f32)
    grad_txt = col0 + both_back.astype(f32) + far_back.astype(f32)

    img_high, img_low = direction(image_unit, image_len, grad_img)
    txt_high, txt_low = direction(text_unit, text_len, grad_txt)
    high_in = swap(jnp.where(first, txt_high, img_high), "core")
    low_in = swap(jnp.where(first, txt_low, img_low), "core")
    high_own = jnp.where(first, img_high, txt_high)
    low_own = jnp.where(first, img_low, txt_low)
    feats2 = jnp.concatenate([kept_feats, feats_in], axis=0)
    high2 = jnp.concatenate([high_own, high_in], axis=0)
    low2 = jnp.concatenate([low_own, low_in], axis=0)
    dims = (((0,), (0,)), ((), ()))
    part = lax.dot_general(feats2, high2, dims, preferred_element_type=f32) + lax.dot_general(
        feats2, low2, dims, preferred_element_type=f32
    )
    own_total, other_total, own_e, other_e = sum_everywhere(part)
    own_total = own_total.astype(f32) * jnp.exp2(own_e)
    other_total = other_total.astype(f32) * jnp.exp2(other_e)
    return (
        jnp.where(first, own_total, other_total),
        jnp.where(first, other_total, own_total),
    )


def solution(mesh):
    fine = Mesh(mesh.devices.reshape(2, 8, 4, 2, 2), AXES)
    rows = P(AXES, None)
    in_specs = (rows, P(), rows, rows, rows, P(), P(), P(AXES))
    return jax.shard_map(
        local, mesh=fine, in_specs=in_specs, out_specs=(P(), P()), check_vma=False
    )
```

```python
import jax
import jax.numpy as jnp
from jax import lax
from jax.sharding import Mesh
from jax.sharding import PartitionSpec as P

epsilon = 1e-06
scale = 20.0
shift = -1.0

AXES = ("yl", "z", "x", "core", "yh")
DP = ("yl", "z", "x", "core")
N_DP = 128

f32 = jnp.float32
bf16 = jnp.bfloat16
f16 = jnp.float16


def unit_rows(raw_rows):
    row_len = jnp.sqrt(jnp.sum(raw_rows * raw_rows, axis=1, keepdims=True) + epsilon)
    return (raw_rows / row_len, row_len)


def swap(block, axis):
    return lax.ppermute(block, axis, [(0, 1), (1, 0)])


def along_dp(block, route):
    return lax.ppermute(block, DP, route)


def chip_shift(block, step):
    return along_dp(block, [(i, (i + 2 * step) % N_DP) for i in range(N_DP)])


def pair_tile(target_rows, image_rows, row_ids, target_cols, text_cols, col_ids):
    teacher_dot = lax.dot_general(
        target_rows, target_cols, (((1,), (1,)), ((), ())), preferred_element_type=f32
    )
    labels = (row_ids[:, None] == col_ids[None, :]).astype(f32)
    target = 0.5 * jax.nn.sigmoid(scale * teacher_dot + shift) + 0.5 * labels
    logits = (
        scale
        * lax.dot_general(
            image_rows, text_cols, (((1,), (1,)), ((), ())), preferred_element_type=f32
        )
        + shift
    )
    scaled = ((jax.nn.sigmoid(logits) - target) / text_cols.shape[0]).astype(bf16)
    row_part = scale * jnp.dot(scaled, text_cols, preferred_element_type=f32)
    col_part = scale * lax.dot_general(
        scaled, image_rows, (((0,), (0,)), ((), ())), preferred_element_type=f32
    )
    return (row_part, col_part)


def direction(unit, length, grad):
    d = (grad - unit * jnp.sum(unit * grad, axis=1, keepdims=True)) / length
    high = d.astype(bf16)
    low = (d - high.astype(f32)).astype(bf16)
    return high, low


def packed(values, exponent):
    scaled = (values * jnp.exp2(-exponent)).astype(f16)
    shape = (values.shape[0], 8, values.shape[2])
    note = jnp.broadcast_to(exponent.astype(f16), shape)
    return jnp.concatenate([scaled, note], axis=1)


def unpacked_sum(blocks):
    exponents = blocks[:, -8:-7, :].astype(f32)
    summed = (blocks[:, :-8].astype(f32) * jnp.exp2(exponents)).sum(axis=0)
    return summed, exponents.max(axis=0)


def sum_everywhere(part):
    ds = part.shape[0]
    biggest = jnp.log2(jnp.maximum(jnp.max(jnp.abs(part)), 1e-30))
    exponent = jnp.clip(jnp.ceil(biggest) - 14.0, -110.0, 110.0)
    blocks = packed(part.reshape(4, ds // 4, ds), exponent)
    blocks = lax.all_to_all(blocks, "x", 0, 0, tiled=True)
    summed, exponent = unpacked_sum(blocks)
    exponent = exponent + 2.0
    blocks = packed(summed.reshape(8, ds // 32, ds), exponent)
    blocks = lax.all_to_all(blocks, "z", 0, 0, tiled=True)
    summed, exponent = unpacked_sum(blocks)
    noted = jnp.concatenate([summed, jnp.broadcast_to(exponent, (8, ds))], axis=0)
    other_l = swap(noted, "yl")
    other_h = swap(noted, "yh")
    other_b = lax.ppermute(noted, ("yl", "yh"), [(0, 3), (1, 2), (2, 1), (3, 0)])
    summed = ((noted + other_l) + (other_h + other_b))[:-8]
    exponent = jnp.maximum(
        jnp.maximum(noted, other_l), jnp.maximum(other_h, other_b)
    )[-8:-7] + 5.0
    other_e = swap(jnp.broadcast_to(exponent, (8, ds)), "core")[0:1]
    block = (summed * jnp.exp2(-exponent)).astype(f16)
    spread = jnp.broadcast_to(block[None], (8,) + block.shape)
    gathered = lax.all_to_all(spread, "z", 0, 0, tiled=True).reshape(ds // 4, ds)
    spread = jnp.broadcast_to(gathered[None], (4,) + gathered.shape)
    own_total = lax.all_to_all(spread, "x", 0, 0, tiled=True).reshape(ds, ds)
    return own_total, swap(own_total, "core"), exponent, other_e


def local(
    teacher_image,
    teacher_proj,
    teacher_text,
    image_feats,
    text_feats,
    image_proj,
    text_proj,
    class_ids,
):
    core = lax.axis_index("core")
    first = core == 0
    back_route = [(i, i - 1 if i % 2 else (i - 3) % N_DP) for i in range(N_DP)]
    step_route = [(i, (i + 1) % N_DP) for i in range(N_DP)]

    ids_y = swap(class_ids, "yh")
    ids1 = along_dp(class_ids, step_route)
    ids2 = along_dp(class_ids, [(i, (i + 2) % N_DP) for i in range(N_DP)])
    ids3 = along_dp(class_ids, [(i, (i + 3) % N_DP) for i in range(N_DP)])

    text_unit, text_len = unit_rows(jnp.dot(text_feats, text_proj, preferred_element_type=f32))
    text_emb = text_unit.astype(bf16)
    text_recv = chip_shift(text_emb, 1)
    image_unit, image_len = unit_rows(
        jnp.dot(image_feats, image_proj, preferred_element_type=f32)
    )
    image_emb = image_unit.astype(bf16)
    image_y = swap(image_emb, "yh")
    teacher_text, text_emb = lax.optimization_barrier((teacher_text, text_emb))
    written_unit, _ = unit_rows(teacher_text.astype(f32))
    teacher_txt = written_unit.astype(bf16)
    teach_recv = chip_shift(teacher_txt, 1)
    teacher_unit, _ = unit_rows(jnp.dot(teacher_image, teacher_proj, preferred_element_type=f32))
    teacher_img = teacher_unit.astype(bf16)
    teach_y = swap(teacher_img, "yh")
    text_exch = swap(text_recv, "core")
    text_far = along_dp(jnp.where(first, text_emb, text_recv), step_route)
    teach_exch = swap(teach_recv, "core")
    teach_far = along_dp(jnp.where(first, teacher_txt, teach_recv), step_route)

    sent_feats = jnp.where(first, text_feats, image_feats)
    kept_feats = jnp.where(first, image_feats, text_feats)
    feats_in = swap(sent_feats, "core")

    image_rows = jnp.concatenate([image_emb, image_y], axis=0)
    teach_rows = jnp.concatenate([teacher_img, teach_y], axis=0)
    row_ids = jnp.concatenate([class_ids, ids_y], axis=0)
    row0, col0 = pair_tile(teach_rows, image_rows, row_ids, teacher_txt, text_emb, class_ids)
    row1, col1 = pair_tile(teach_rows, image_rows, row_ids, teach_recv, text_recv, ids2)
    ids_exch = jnp.where(first, ids1, ids3)
    row2, col2 = pair_tile(teach_rows, image_rows, row_ids, teach_exch, text_exch, ids_exch)
    both = col1 + swap(col2.astype(bf16), "core").astype(f32)
    both_back = chip_shift(both.astype(bf16), -1)
    ids_far = jnp.where(first, ids3, ids1)
    row3, col3 = pair_tile(teach_rows, image_rows, row_ids, teach_far, text_far, ids_far)
    far_back = along_dp(col3.astype(bf16), back_route)
    grad_rows = row0 + row1 + row2 + row3
    half = text_emb.shape[0]
    rows_y = swap(grad_rows[half:].astype(bf16), "yh")
    grad_img = grad_rows[:half] + rows_y.astype(f32)
    grad_txt = col0 + both_back.astype(f32) + far_back.astype(f32)

    img_high, img_low = direction(image_unit, image_len, grad_img)
    txt_high, txt_low = direction(text_unit, text_len, grad_txt)
    high_in = swap(jnp.where(first, txt_high, img_high), "core")
    low_in = swap(jnp.where(first, txt_low, img_low), "core")
    high_own = jnp.where(first, img_high, txt_high)
    low_own = jnp.where(first, img_low, txt_low)
    feats2 = jnp.concatenate([kept_feats, feats_in], axis=0)
    high2 = jnp.concatenate([high_own, high_in], axis=0)
    low2 = jnp.concatenate([low_own, low_in], axis=0)
    dims = (((0,), (0,)), ((), ()))
    part = lax.dot_general(feats2, high2, dims, preferred_element_type=f32) + lax.dot_general(
        feats2, low2, dims, preferred_element_type=f32
    )
    own_total, other_total, own_e, other_e = sum_everywhere(part)
    own_total = own_total.astype(f32) * jnp.exp2(own_e)
    other_total = other_total.astype(f32) * jnp.exp2(other_e)
    return (
        jnp.where(first, own_total, other_total),
        jnp.where(first, other_total, own_total),
    )


def solution(mesh):
    fine = Mesh(mesh.devices.reshape(2, 8, 4, 2, 2), AXES)
    rows = P(AXES, None)
    in_specs = (rows, P(), rows, rows, rows, P(), P(), P(AXES))
    return jax.shard_map(
        local, mesh=fine, in_specs=in_specs, out_specs=(P(), P()), check_vma=False
    )
```
